256 devices in a mesh: heads: 16 (over y_hi, x, core), seq: 16 (over z, y_lo).
Axes of the slice: x: 4, y: 4 (y_hi: 2, y_lo: 2; y = y_hi * 2 + y_lo), z: 8, core: 2. Of those that a mesh axis runs over, the one named last changes fastest.
Arguments:
- queries: bfloat16 [4096, 2048], P('seq', 'heads'), may hold values from -250 to 250
- key_rows: bfloat16 [4096, 256], P('seq'), may hold values from -4 to 4
- value_rows: bfloat16 [4096, 256], P('seq'), may hold values from -4 to 4
- layer_grad: bfloat16 [4096, 8192], P('seq', 'heads'), may hold values from -6 to 6
- w_out: bfloat16 [2048, 8192], P(None, 'heads'), may hold values from -0.09375 to 0.09375
- block_order: int32 [32], replicated, may hold values from 0 to 31, each once
- doc_lengths: int32 [4], replicated, may hold values from 1 to 2048, 4096 in all
Outputs:
- query_grad: bfloat16 [4096, 2048], P('seq', 'heads')
- key_grad: bfloat16 [4096, 256], P('seq')
- value_grad: bfloat16 [4096, 256], P('seq')
- head_grad: bfloat16 [4096, 2048], P('seq', 'heads')
The draws below stay inside these ranges and needn't reach their ends.
Inputs may be any that keep to these rules, and one draw needn't show every extreme that they name: `block_order`: a permutation of the (32) sequence blocks. `doc_lengths`: the documents' lengths sum to 4096; the longest holds half of 4096.
All inputs are finite; a program needn't handle non-finite values.
Results may differ from the reference program's by a relative error of at most 0.03.
Values may be sent and summed in bfloat16 or wider, within the bound.
A program may use at most 64 MiB of HBM per device.

```python
import math
import jax
import jax.numpy as jnp
import numpy as np
from jax import lax

D = 8192
DH = 128
GROUP = 8
BLOCK = 128
NDOC = 4
QHEADS = 16
KVHEADS = 2
SEQ = 4096
N_HEADS = 16
N_SEQ = 16


def shared_keys(key, bound):
    normal_base = jnp.clip(jax.random.normal(key, (SEQ, KVHEADS * DH), jnp.float32), -bound, bound)
    row_ids = jnp.arange(SEQ)
    chosen = (row_ids % 61 == 7)[:, None]
    before = jnp.roll(chosen, -1, axis=0)
    mixed = jnp.where(before, normal_base, normal_base)
    return mixed


def draw_key_rows(key, part):
    mixed = shared_keys(key, 4.0)
    return mixed.astype(jnp.bfloat16)


def draw_queries(key, part):
    key = jax.random.fold_in(key, 11)
    key_noise = jax.random.fold_in(key, 0)
    noise_rows = jnp.clip(jax.random.normal(key_noise, (SEQ, QHEADS * DH), jnp.float32), -4.0, 4.0)
    return noise_rows.astype(jnp.bfloat16)


def with_spikes(entries, stream_key, source, target, blocks, factor):
    def block_of(dim):
        return (jnp.arange(entries.shape[dim]) // (entries.shape[dim] // blocks)).reshape((-1,) + (1,) * (entries.ndim - 1 - dim))

    near = jax.random.permutation(stream_key, blocks)[block_of(target)]
    far = (block_of(target) + blocks // 2) % blocks
    return jnp.where((block_of(source) == near) | (block_of(source) == far), factor * entries, entries)


def block_scale(own_key, dims, cuts, least, top_value):
    def one(dim, shards_of):
        draws = jax.random.uniform(jax.random.fold_in(jax.random.fold_in(own_key, 6), dim), (shards_of,), jnp.float32, least / len(cuts), top_value / len(cuts))
        return jnp.repeat(jnp.exp(draws), dims[dim] // shards_of).reshape((-1,) + (1,) * (len(dims) - dim - 1))

    level = one(*cuts[0])
    for cut in cuts[1:]:
        level = level * one(*cut)
    return level


def length_profile(amount, total, reach, lean):
    weights = [(1 << 20) // math.isqrt(rank ** lean) + 1 for rank in range(2, amount + 1)]
    rest, given = total - reach - (amount - 1), [1] * (amount - 1)
    while rest > 0:
        free = [i for i in range(amount - 1) if given[i] < reach]
        pool, left = sum([weights[i] for i in free]), rest
        for i in free:
            addition = min(reach - given[i], max(1, left * weights[i] // pool), rest)
            given[i] = given[i] + addition
            rest = rest - addition
    return np.array([reach] + given)


def ragged_sizes(rng, amount, total, limit, skew):
    if amount == 2:
        one = jax.random.randint(rng, (), max(1, total - limit), min(limit, total - 1) + 1)
        return jnp.stack([one, total - one])
    lengths = jnp.asarray(length_profile(amount, total, limit, skew), jnp.int32)
    couples = (amount - 1) // 2
    source_of, receiver = lengths[1:1 + 2 * couples:2], lengths[2:2 + 2 * couples:2]
    room = jnp.minimum(source_of - 1, limit - receiver)
    moved = jax.random.randint(jax.random.fold_in(rng, 1), (couples,), 0, 1 << 20) % (room + 1)
    lengths = lengths.at[1:1 + 2 * couples:2].set(source_of - moved).at[2:2 + 2 * couples:2].set(receiver + moved)
    return lengths[jax.random.permutation(jax.random.fold_in(rng, 2), amount)]


def noise(stream_key, extent, deviation, most, cuts=(), held_as=jnp.bfloat16):
    result = jax.random.normal(stream_key, extent, jnp.float32) * deviation
    if len(cuts) > 0:
        result = block_scale(stream_key, extent, cuts, -0.22, 0.18) * result
    return jnp.clip(result, min=-most, max=most).astype(held_as)


def gaussian_with(key, shape, spread, limit, cuts, heavy, held_as=jnp.bfloat16):
    result = spread * jax.random.normal(key, shape, jnp.float32)
    if cuts:
        result = result * block_scale(key, shape, cuts, -0.22, 0.18)
    return jnp.clip(with_spikes(result, jax.random.fold_in(key, 3), *heavy), -limit, limit).astype(held_as)


def setup_inputs(seed: int = 0) -> dict:
    streams_of = jax.random.split(jax.random.key(seed), 8)
    return {
        "queries": draw_queries(jax.random.fold_in(streams_of[7], 71), 0),
        "key_rows": draw_key_rows(jax.random.fold_in(streams_of[7], 71), 0),
        "value_rows": noise(streams_of[2], (SEQ, KVHEADS * DH), 1.0, 4.0, ((0, 16),)),
        "layer_grad": noise(streams_of[3], (SEQ, D), 1.0, 6.0, ((0, 16), (1, 16))),
        "w_out": gaussian_with(streams_of[4], (QHEADS * DH, D), D ** -0.5, 0.09375, ((1, 16),), (1, 0, 16, 2.0)),
        "block_order": jax.random.permutation(streams_of[5], 2 * N_SEQ).astype(jnp.int32),
        "doc_lengths": ragged_sizes(streams_of[6], NDOC, SEQ, SEQ // 2, 0).astype(jnp.int32),
    }


neg_large = -1e+30

def doc_begin(positions, doc_lengths):
    starts = (jnp.cumsum(doc_lengths) - doc_lengths).astype(jnp.int32)
    inside = starts[None, :] <= positions[:, None]
    return lax.optimization_barrier(jnp.max(jnp.where(inside, starts[None, :], 0), axis=1)).astype(jnp.int32)

def contract_last(left, right):
    return lax.dot_general(left, right, (((1,), (1,)), ((), ())), preferred_element_type=jnp.float32)

def contract_first(left, right):
    return lax.dot_general(left, right, (((0,), (0,)), ((), ())), preferred_element_type=jnp.float32)

def reference(queries, key_rows, value_rows, layer_grad, w_out, block_order, doc_lengths):
    shard_width = D // N_HEADS

    def add_shard(summed, shard_index):
        part_grad = lax.dynamic_slice_in_dim(layer_grad, shard_index * shard_width, shard_width, 1)
        part_weight = lax.dynamic_slice_in_dim(w_out, shard_index * shard_width, shard_width, 1)
        rounded = contract_last(part_grad, part_weight).astype(jnp.bfloat16)
        rounded = lax.optimization_barrier(rounded)
        return (summed + rounded.astype(jnp.float32), None)
    summed, _ = lax.scan(add_shard, jnp.zeros((SEQ, QHEADS * DH), jnp.float32), jnp.arange(N_HEADS, dtype=jnp.int32))
    head_grad = summed.astype(jnp.bfloat16)
    row_ids = jnp.arange(SEQ, dtype=jnp.int32)
    positions = (block_order[row_ids // BLOCK] * BLOCK + row_ids % BLOCK).astype(jnp.int32)
    begins = doc_begin(positions, doc_lengths)
    score_scale = 1.0 / math.sqrt(DH)

    def per_head(loop_state, head_index):
        key_all, value_all = loop_state
        shared_head = (head_index // GROUP).astype(jnp.int32)
        head_queries = lax.dynamic_slice_in_dim(queries, head_index * DH, DH, 1)
        head_outgrad = lax.dynamic_slice_in_dim(head_grad, head_index * DH, DH, 1)
        head_keys = lax.dynamic_slice_in_dim(key_rows, shared_head * DH, DH, 1)
        head_values = lax.dynamic_slice_in_dim(value_rows, shared_head * DH, DH, 1)
        wide_values = head_values.astype(jnp.float32)

        def per_block(partial_value, block_index):
            key_part, value_part = partial_value
            first_row = block_index * BLOCK
            block_queries = lax.dynamic_slice_in_dim(head_queries, first_row, BLOCK, 0)
            block_outgrad = lax.dynamic_slice_in_dim(head_outgrad, first_row, BLOCK, 0)
            block_pos = lax.dynamic_slice_in_dim(positions, first_row, BLOCK, 0)
            block_begin = lax.dynamic_slice_in_dim(begins, first_row, BLOCK, 0)
            allowed = (positions[None, :] <= block_pos[:, None]) & (positions[None, :] >= block_begin[:, None])
            scores = jnp.where(allowed, contract_last(block_queries, head_keys) * score_scale, neg_large)
            row_top = lax.optimization_barrier(jnp.max(scores, axis=1))
            weights = jnp.where(allowed, jnp.exp(scores - row_top[:, None]), 0.0)
            row_sum = lax.optimization_barrier(jnp.sum(weights, axis=1))
            attended = jnp.dot(weights, wide_values, precision=lax.Precision.HIGHEST) / row_sum[:, None]
            log_norm = row_top + jnp.log(row_sum)
            row_dots = lax.optimization_barrier(jnp.sum(block_outgrad.astype(jnp.float32) * attended, axis=1))
            probabilities = jnp.where(allowed, jnp.exp(scores - log_norm[:, None]), 0.0)
            value_part = value_part + contract_first(probabilities.astype(jnp.bfloat16), block_outgrad)
            dprobs = contract_last(block_outgrad, head_values)
            dscores = (probabilities * (dprobs - row_dots[:, None])).astype(jnp.bfloat16)
            query_part = jnp.dot(dscores, head_keys, preferred_element_type=jnp.float32) * score_scale
            key_part = key_part + contract_first(dscores, block_queries)
            return ((key_part, value_part), query_part)
        empty = jnp.zeros((SEQ, DH), jnp.float32)
        (key_part, value_part), query_parts = lax.scan(per_block, (empty, empty), jnp.arange(SEQ // BLOCK, dtype=jnp.int32))
        old_keys = lax.dynamic_slice_in_dim(key_all, shared_head * DH, DH, 1)
        old_values = lax.dynamic_slice_in_dim(value_all, shared_head * DH, DH, 1)
        key_all = lax.dynamic_update_slice_in_dim(key_all, old_keys + key_part * score_scale, shared_head * DH, 1)
        value_all = lax.dynamic_update_slice_in_dim(value_all, old_values + value_part, shared_head * DH, 1)
        return ((key_all, value_all), query_parts.reshape(SEQ, DH))
    start_state = (jnp.zeros((SEQ, KVHEADS * DH), jnp.float32), jnp.zeros((SEQ, KVHEADS * DH), jnp.float32))
    (key_all, value_all), query_parts = lax.scan(per_head, start_state, jnp.arange(QHEADS, dtype=jnp.int32))
    query_grad = jnp.transpose(query_parts, (1, 0, 2)).reshape(SEQ, QHEADS * DH)
    return (query_grad.astype(jnp.bfloat16), key_all.astype(jnp.bfloat16), value_all.astype(jnp.bfloat16), head_grad)
```

```python
import math

import jax
import jax.numpy as jnp
from jax import lax
from jax.experimental import pallas as pl
from jax.experimental.pallas import tpu as pltpu
from jax.sharding import PartitionSpec as P

GROUP = 8
DH = 128
ROWS = 256
MESH = pl.DeviceIdType.MESH
F32 = jnp.float32
BF16 = jnp.bfloat16
NEG = -1e30


def contract_last(left, right):
    return lax.dot_general(
        left, right, (((1,), (1,)), ((), ())), preferred_element_type=F32
    )


def matmul(left, right):
    return jnp.dot(left, right, preferred_element_type=F32)


def make_kernel(n_seq):
    part = ROWS // GROUP
    keys = n_seq * part
    n_heads = 2 * GROUP
    chips = n_heads // 2
    scale = 1.0 / math.sqrt(DH)
    scale2 = scale * math.log2(math.e)

    def kernel(
        q_hbm, k_hbm, v_hbm, lg_hbm, w_hbm, bo, dl,
        qg_out, kg_out, vg_out, hg_out,
        w_v, lg_v, q_all, do_all, kv_own, kv_all, kt_v, bias,
        mine, oth_tx, oth_rx, c1_tx, c1_rx,
        e_all, dp_all, st_own, st_rx, fac, ds_own, ds_rx, dsum,
        dv_acc, dk_acc, dv_tx, dk_tx, dv_rx, dk_rx, dv_fin, dk_fin,
        dq_tx, dq_rx, qg_v,
        w_sem, ld_sem, out_sem,
        q_send, q_recv, kv_send, kv_recv, oth_send, oth_recv, c1_send, c1_recv,
        do_send, do_recv, st_send, st_recv, d_send, d_recv, dq_send, dq_recv,
        dv_send, dv_recv, dk_send, dk_recv, av_send, av_recv, ak_send, ak_recv,
    ):
        h = lax.axis_index("heads")
        s = lax.axis_index("seq")
        c = h // GROUP
        j = h % GROUP
        x = j // 2
        core = h % 2
        chip = h // 2
        sib = h + 1 - 2 * core

        def to_head(src, dst, send_sem, recv_sem, target):
            return pltpu.make_async_remote_copy(
                src_ref=src, dst_ref=dst, send_sem=send_sem, recv_sem=recv_sem,
                device_id={"heads": target}, device_id_type=MESH,
            )

        def to_seq(src, dst, send_sem, recv_sem, target):
            return pltpu.make_async_remote_copy(
                src_ref=src, dst_ref=dst, send_sem=send_sem, recv_sem=recv_sem,
                device_id={"seq": target}, device_id_type=MESH,
            )

        def await_bytes(ref, sem):
            pltpu.make_async_copy(ref, ref, sem).wait()

        row0 = pl.multiple_of(j * part, part)
        col0 = pl.multiple_of(c * DH, DH)
        lg_load = pltpu.make_async_copy(lg_hbm, lg_v, ld_sem.at[0])
        q_load = pltpu.make_async_copy(q_hbm, q_all.at[j], ld_sem.at[1])
        k_load = pltpu.make_async_copy(
            k_hbm.at[pl.ds(row0, part), pl.ds(col0, DH)],
            kv_own.at[:, pl.ds(0, DH)], ld_sem.at[2],
        )
        v_load = pltpu.make_async_copy(
            v_hbm.at[pl.ds(row0, part), pl.ds(col0, DH)],
            kv_own.at[:, pl.ds(DH, DH)], ld_sem.at[3],
        )
        q_load.start()
        k_load.start()
        v_load.start()
        lg_load.start()

        def w_load(step, which):
            target = ((chip + step + 1) % chips) * 2
            head = target + core if which == 0 else target + 1 - core
            return pltpu.make_async_copy(
                w_hbm.at[pl.ds(pl.multiple_of(head * DH, DH), DH), :],
                w_v.at[step, pl.ds(which * DH, DH), :],
                w_sem.at[step, which],
            )

        for step in range(chips):
            for which in range(2):
                w_load(step, which).start()

        barrier = pltpu.get_barrier_semaphore()
        for r in range(1, n_heads):
            pl.semaphore_signal(
                barrier, inc=1, device_id={"heads": (h + r) % n_heads}, device_id_type=MESH
            )
        for r in range(1, n_seq):
            pl.semaphore_signal(
                barrier, inc=1, device_id={"seq": (s + r) % n_seq}, device_id_type=MESH
            )

        lane = lax.broadcasted_iota(jnp.int32, (1, ROWS), 1)
        q_pos = jnp.where(
            lane < ROWS // 2,
            bo[2 * s] * (ROWS // 2) + lane,
            bo[2 * s + 1] * (ROWS // 2) + lane - ROWS // 2,
        )
        start1 = dl[0]
        start2 = start1 + dl[1]
        start3 = start2 + dl[2]
        q_begin = jnp.zeros((1, ROWS), jnp.int32)
        for begin in (start1, start2, start3):
            q_begin = jnp.maximum(q_begin, jnp.where(begin <= q_pos, begin, 0))

        def bias_step(r, carry):
            slot = (s - r + n_seq) % n_seq
            base = bo[2 * slot + j // 4] * (ROWS // 2) + (j % 4) * part
            k_pos = base + lax.broadcasted_iota(jnp.int32, (part, ROWS), 0)
            allowed = (k_pos <= q_pos) & (k_pos >= q_begin)
            bias[pl.ds(pl.multiple_of(r * part, part), part), :] = jnp.where(allowed, 0.0, NEG)
            return carry

        lax.fori_loop(0, n_seq, bias_step, 0)
        q_load.wait()
        k_load.wait()
        v_load.wait()
        pl.semaphore_wait(barrier, n_heads + n_seq - 2)

        def peer(t, q):
            return ((x - t + 4) % 4) * 2 + (core + q) % 2

        def gather_first(buf, send, recv):
            for t in (2, 1, 3):
                to_head(
                    buf.at[j], buf.at[j], send.at[2 * t], recv.at[2 * t],
                    c * GROUP + ((x + t) % 4) * 2 + core,
                ).start()
            to_head(buf.at[j], buf.at[j], send.at[1], recv.at[1], sib).start()

        def gather_wait(buf, recv, t, q):
            ref = buf.at[peer(t, q)]
            pltpu.make_async_copy(ref, ref, recv.at[2 * t + q]).wait()

        def gather_pass(buf, send, recv, t):
            gather_wait(buf, recv, t, 0)
            other = peer(t, 0)
            to_head(
                buf.at[other], buf.at[other], send.at[2 * t + 1], recv.at[2 * t + 1], sib
            ).start()

        gather_first(q_all, q_send, q_recv)

        def kv_step(r, carry):
            to_seq(
                kv_own, kv_all.at[pl.ds(pl.multiple_of(r * part, part), part), :],
                kv_send, kv_recv, (s + r) % n_seq,
            ).start()
            return carry

        lax.fori_loop(1, n_seq, kv_step, 0)
        kv_all[pl.ds(0, part), :] = kv_own[...]

        lg_load.wait()

        def c1_copy(i):
            target = ((chip + i + 1) % chips) * 2 + core
            return to_head(c1_tx.at[i], c1_rx.at[i], c1_send.at[i], c1_recv, target)

        def product_step(i, carry):
            @pl.when(i < chips)
            def _():
                for which in range(2):
                    pltpu.make_async_copy(
                        w_v.at[i, pl.ds(which * DH, DH), :],
                        w_v.at[i, pl.ds(which * DH, DH), :],
                        w_sem.at[i, which],
                    ).wait()
                product = contract_last(lg_v[...], w_v[i])
                oth_tx[i] = product[:, DH:].astype(BF16)
                to_head(oth_tx.at[i], oth_rx.at[i], oth_send.at[i], oth_recv.at[i], sib).start()
                mine[i] = product[:, :DH]

            @pl.when(i >= 2)
            def _():
                k = i - 2
                pltpu.make_async_copy(oth_rx.at[k], oth_rx.at[k], oth_recv.at[k]).wait()
                total = mine[k] + oth_rx[k].astype(F32)

                @pl.when(k < chips - 1)
                def _():
                    c1_tx[k] = total.astype(BF16)
                    c1_copy(k).start()

                @pl.when(k == chips - 1)
                def _():
                    mine[k] = total

            return carry

        lax.fori_loop(0, chips + 2, product_step, 0)

        for t in (1, 3, 2):
            gather_pass(q_all, q_send, q_recv, t)

        await_bytes(kv_all.at[pl.ds(part, keys - part), :], kv_recv)
        kt_v[...] = kv_all[:, :DH].astype(F32).T.astype(BF16)

        def score_head(head):
            sc = contract_last(kv_all[:, :DH], q_all[head]) * scale2 + bias[...]
            top = jnp.max(sc, axis=0, keepdims=True)
            e = jnp.exp2(sc - top)
            e_all[head] = e
            st_own[0, pl.ds(head, 1), :] = top
            st_own[1, pl.ds(head, 1), :] = jnp.sum(e, axis=0, keepdims=True)

        order = ((0, 0), (0, 1), (1, 0), (3, 0), (2, 0), (1, 1), (3, 1), (2, 1))
        for t, q in order:
            if q == 1:
                gather_wait(q_all, q_recv, t, q)
            score_head(peer(t, q))

        for r in range(1, GROUP):
            to_head(
                st_own, st_rx.at[r - 1], st_send, st_recv, c * GROUP + (j + r) % GROUP
            ).start()

        await_bytes(c1_rx, c1_recv)
        total = mine[chips - 1]
        for i in range(chips - 1):
            total = total + c1_rx[i].astype(F32)
        do_all[j] = total.astype(BF16)
        gather_first(do_all, do_send, do_recv)
        hg_copy = pltpu.make_async_copy(do_all.at[j], hg_out, out_sem.at[0])
        hg_copy.start()

        await_bytes(st_rx, st_recv)
        top = st_own[0]
        for r in range(GROUP - 1):
            top = jnp.maximum(top, st_rx[r, 0])
        norm = st_own[1] * jnp.exp2(st_own[0] - top)
        for r in range(GROUP - 1):
            norm = norm + st_rx[r, 1] * jnp.exp2(st_rx[r, 0] - top)
        fac[...] = jnp.exp2(st_own[0] - top) / norm

        dv_acc[...] = jnp.zeros_like(dv_acc)

        def value_head(head):
            p = e_all[head] * fac[pl.ds(head, 1), :]
            e_all[head] = p
            dp = contract_last(kv_all[:, DH:], do_all[head])
            dp_all[head] = dp
            ds_own[pl.ds(head, 1), :] = jnp.sum(p * dp, axis=0, keepdims=True)
            dv_acc[...] += matmul(p.astype(BF16), do_all[head])

        for t, q in order:
            if t > 0 and q == 0:
                gather_pass(do_all, do_send, do_recv, t)
            elif q == 1:
                gather_wait(do_all, do_recv, t, q)
            value_head(peer(t, q))

        for r in range(1, GROUP):
            to_head(
                ds_own, ds_rx.at[r - 1], d_send, d_recv, c * GROUP + (j + r) % GROUP
            ).start()

        dv_tx[...] = dv_acc[...].astype(BF16)

        def scatter(tx, rx, send, recv):
            def step(r, carry):
                rows = pl.ds(pl.multiple_of(r * part, part), part)
                to_seq(
                    tx.at[rows, :], rx.at[rows, :], send, recv, (s - r + n_seq) % n_seq
                ).start()
                return carry

            lax.fori_loop(1, n_seq, step, 0)

        scatter(dv_tx, dv_rx, dv_send, dv_recv)

        await_bytes(ds_rx, d_recv)
        total_d = ds_own[...]
        for r in range(GROUP - 1):
            total_d = total_d + ds_rx[r]
        dsum[...] = total_d

        dk_acc[...] = jnp.zeros_like(dk_acc)

        def grad_head(head):
            ds = (e_all[head] * (dp_all[head] - dsum[pl.ds(head, 1), :])).astype(BF16)
            dq_tx[head] = (matmul(kt_v[...], ds) * scale).astype(BF16)
            dk_acc[...] += matmul(ds, q_all[head])

        def dq_copy(t, q):
            head = peer(t, q)
            slot = 2 * t + q - 1
            return to_head(
                dq_tx.at[head], dq_rx.at[slot], dq_send.at[slot], dq_recv, c * GROUP + head
            )

        for t, q in ((2, 0), (2, 1), (1, 0), (1, 1), (3, 0), (3, 1), (0, 1), (0, 0)):
            grad_head(peer(t, q))
            if (t, q) != (0, 0):
                dq_copy(t, q).start()

        dk_tx[...] = (dk_acc[...] * scale).astype(BF16)
        scatter(dk_tx, dk_rx, dk_send, dk_recv)

        def finish(tx, rx, fin, out, recv, all_send, all_recv, own_sem):
            await_bytes(rx.at[pl.ds(part, keys - part), :], recv)
            summed = tx[pl.ds(0, part), :].astype(F32)
            for r in range(1, n_seq):
                summed = summed + rx[pl.ds(r * part, part), :].astype(F32)
            fin[...] = summed.astype(BF16)
            place = out.at[pl.ds(row0, part), pl.ds(col0, DH)]

            def step(r, carry):
                to_head(fin, place, all_send, all_recv, (h + r) % n_heads).start()
                return carry

            lax.fori_loop(1, n_heads, step, 0)
            pltpu.make_async_copy(fin, place, own_sem).start()

        finish(dv_tx, dv_rx, dv_fin, vg_out, dv_recv, av_send, av_recv, out_sem.at[1])
        finish(dk_tx, dk_rx, dk_fin, kg_out, dk_recv, ak_send, ak_recv, out_sem.at[2])

        await_bytes(dq_rx, dq_recv)
        query_sum = dq_tx[j].astype(F32)
        for r in range(GROUP - 1):
            query_sum = query_sum + dq_rx[r].astype(F32)
        qg_v[...] = query_sum.T.astype(BF16)
        qg_copy = pltpu.make_async_copy(qg_v, qg_out, out_sem.at[3])
        qg_copy.start()

        for slot in range(1, 2 * 4):
            await_bytes(q_all.at[0], q_send.at[slot])
            await_bytes(do_all.at[0], do_send.at[slot])
        await_bytes(kv_all.at[pl.ds(part, keys - part), :], kv_send)
        for i in range(chips):
            await_bytes(oth_tx.at[i], oth_send.at[i])
        for i in range(chips - 1):
            await_bytes(c1_tx.at[i], c1_send.at[i])
        await_bytes(st_rx, st_send)
        await_bytes(ds_rx, d_send)
        for slot in range(GROUP - 1):
            await_bytes(dq_tx.at[0], dq_send.at[slot])
        for tx, send in ((dv_tx, dv_send), (dk_tx, dk_send)):
            await_bytes(tx.at[pl.ds(part, keys - part), :], send)
        spread = (n_heads - 1) * part
        for sem in (av_send, ak_send, av_recv, ak_recv):
            await_bytes(q_all.at[pl.ds(0, 5), pl.ds(0, spread // 5), :], sem)
        hg_copy.wait()
        qg_copy.wait()
        for out, fin, index in ((vg_out, dv_fin, 1), (kg_out, dk_fin, 2)):
            place = out.at[pl.ds(row0, part), pl.ds(col0, DH)]
            pltpu.make_async_copy(fin, place, out_sem.at[index]).wait()

    return kernel


def local(queries, key_rows, value_rows, layer_grad, w_out, block_order, doc_lengths):
    n_seq = lax.axis_size("seq")
    part = ROWS // GROUP
    keys = n_seq * part
    depth = layer_grad.shape[1]
    chips = GROUP
    vmem = pltpu.VMEM
    dma = pltpu.SemaphoreType.DMA
    scratch = [
        vmem((chips, 2 * DH, depth), BF16),
        vmem((ROWS, depth), BF16),
        vmem((GROUP, ROWS, DH), BF16),
        vmem((GROUP, ROWS, DH), BF16),
        vmem((part, 2 * DH), BF16),
        vmem((keys, 2 * DH), BF16),
        vmem((DH, keys), BF16),
        vmem((keys, ROWS), F32),
        vmem((chips, ROWS, DH), F32),
        vmem((chips, ROWS, DH), BF16),
        vmem((chips, ROWS, DH), BF16),
        vmem((chips - 1, ROWS, DH), BF16),
        vmem((chips - 1, ROWS, DH), BF16),
        vmem((GROUP, keys, ROWS), F32),
        vmem((GROUP, keys, ROWS), F32),
        vmem((2, GROUP, ROWS), F32),
        vmem((GROUP - 1, 2, GROUP, ROWS), F32),
        vmem((GROUP, ROWS), F32),
        vmem((GROUP, ROWS), F32),
        vmem((GROUP - 1, GROUP, ROWS), F32),
        vmem((GROUP, ROWS), F32),
        vmem((keys, DH), F32),
        vmem((keys, DH), F32),
        vmem((keys, DH), BF16),
        vmem((keys, DH), BF16),
        vmem((keys, DH), BF16),
        vmem((keys, DH), BF16),
        vmem((part, DH), BF16),
        vmem((part, DH), BF16),
        vmem((GROUP, DH, ROWS), BF16),
        vmem((GROUP - 1, DH, ROWS), BF16),
        vmem((ROWS, DH), BF16),
        dma((chips, 2)),
        dma((4,)),
        dma((4,)),
        dma((8,)),
        dma((8,)),
        dma,
        dma,
        dma((chips,)),
        dma((chips,)),
        dma((chips - 1,)),
        dma,
        dma((8,)),
        dma((8,)),
        dma,
        dma,
        dma,
        dma,
        dma((GROUP - 1,)),
        dma,
        dma,
        dma,
        dma,
        dma,
        dma,
        dma,
        dma,
        dma,
    ]
    anywhere = pl.BlockSpec(memory_space=pl.ANY)
    scalars = pl.BlockSpec(memory_space=pltpu.SMEM)
    return pl.pallas_call(
        make_kernel(n_seq),
        out_shape=(
            jax.ShapeDtypeStruct(queries.shape, BF16),
            jax.ShapeDtypeStruct(key_rows.shape, BF16),
            jax.ShapeDtypeStruct(value_rows.shape, BF16),
            jax.ShapeDtypeStruct(queries.shape, BF16),
        ),
        in_specs=[anywhere] * 5 + [scalars] * 2,
        out_specs=(anywhere,) * 4,
        scratch_shapes=scratch,
        compiler_params=pltpu.CompilerParams(
            collective_id=0, has_side_effects=True, vmem_limit_bytes=40 * 1024 * 1024
        ),
    )(queries, key_rows, value_rows, layer_grad, w_out, block_order, doc_lengths)


def solution(mesh):
    return jax.shard_map(
        local,
        mesh=mesh,
        in_specs=(
            P("seq", "heads"),
            P("seq", None),
            P("seq", None),
            P("seq", "heads"),
            P(None, "heads"),
            P(),
            P(),
        ),
        out_specs=(P("seq", "heads"), P("seq", None), P("seq", None), P("seq", "heads")),
        check_vma=False,
    )
```

```python
import math

import jax
import jax.numpy as jnp
from jax import lax
from jax.experimental import pallas as pl
from jax.experimental.pallas import tpu as pltpu
from jax.sharding import PartitionSpec as P

GROUP = 8
DH = 128
ROWS = 256
MESH = pl.DeviceIdType.MESH
F32 = jnp.float32
BF16 = jnp.bfloat16
NEG = -1e30


def contract_last(left, right):
    return lax.dot_general(
        left, right, (((1,), (1,)), ((), ())), preferred_element_type=F32
    )


def matmul(left, right):
    return jnp.dot(left, right, preferred_element_type=F32)


def make_kernel(n_seq):
    part = ROWS // GROUP
    keys = n_seq * part
    n_heads = 2 * GROUP
    chips = n_heads // 2
    scale = 1.0 / math.sqrt(DH)
    scale2 = scale * math.log2(math.e)

    def kernel(
        q_hbm, k_hbm, v_hbm, lg_hbm, w_hbm, bo_hbm, dl_hbm,
        qg_out, kg_out, vg_out, hg_out,
        w_v, lg_v, q_all, do_all, k_all, v_all, kt_v, bias, bo, dl,
        mine, oth_tx, oth_rx, c1_tx, c1_rx,
        e_all, dp_all, ds_all, st_own, st_rx, d_own, d_rx, fac, dsum,
        dv_acc, dk_acc, dv_tx, dk_tx, dv_rx, dk_rx, dv_fin, dk_fin,
        dq_tx, dq_rx, qg_v,
        w_sem, ld_sem, out_sem,
        q_send, q_recv, k_send, k_recv, v_send, v_recv, oth_send, oth_recv, c1_send, c1_recv,
        do_send, do_recv, st_send, st_recv, d_send, d_recv, dq_send, dq_recv,
        dv_send, dv_recv, dk_send, dk_recv, av_send, av_recv, ak_send, ak_recv,
    ):
        h = lax.axis_index("heads")
        s = lax.axis_index("seq")
        c = h // GROUP
        j = h % GROUP
        x = j // 2
        core = h % 2
        chip = h // 2
        sib = h + 1 - 2 * core
        seq_order = sorted(range(1, n_seq), key=lambda r: abs(2 * r - n_seq))
        chip_order = (6, 2, 5, 7, 4, 1, 3, 0)
        rest = pl.ds(part, keys - part)

        def to_head(src, dst, send_sem, recv_sem, target):
            return pltpu.make_async_remote_copy(
                src_ref=src, dst_ref=dst, send_sem=send_sem, recv_sem=recv_sem,
                device_id={"heads": target}, device_id_type=MESH,
            )

        def to_seq(src, dst, send_sem, recv_sem, target):
            return pltpu.make_async_remote_copy(
                src_ref=src, dst_ref=dst, send_sem=send_sem, recv_sem=recv_sem,
                device_id={"seq": target}, device_id_type=MESH,
            )

        def await_bytes(ref, sem):
            pltpu.make_async_copy(ref, ref, sem).wait()

        row0 = pl.multiple_of(j * part, part)
        col0 = pl.multiple_of(c * DH, DH)
        own_rows = pl.ds(0, part)
        lg_load = pltpu.make_async_copy(lg_hbm, lg_v, ld_sem.at[0])
        lg_load.start()
        w_loads = []
        for step, r in enumerate(chip_order):
            target = ((chip + r) % chips) * 2
            for which, head in enumerate((target + core, target + 1 - core)):
                load = pltpu.make_async_copy(
                    w_hbm.at[pl.ds(pl.multiple_of(head * DH, DH), DH), :],
                    w_v.at[step, pl.ds(which * DH, DH), :],
                    w_sem.at[step, which],
                )
                load.start()
                w_loads.append(load)
        small_loads = [
            pltpu.make_async_copy(q_hbm, q_all.at[j], ld_sem.at[1]),
            pltpu.make_async_copy(
                k_hbm.at[pl.ds(row0, part), pl.ds(col0, DH)], k_all.at[own_rows, :], ld_sem.at[2]
            ),
            pltpu.make_async_copy(
                v_hbm.at[pl.ds(row0, part), pl.ds(col0, DH)], v_all.at[own_rows, :], ld_sem.at[3]
            ),
            pltpu.make_async_copy(bo_hbm, bo, ld_sem.at[4]),
            pltpu.make_async_copy(dl_hbm, dl, ld_sem.at[5]),
        ]
        for load in small_loads:
            load.start()

        barrier = pltpu.get_barrier_semaphore()
        for r in seq_order:
            pl.semaphore_signal(
                barrier, inc=1, device_id={"seq": (s + r) % n_seq}, device_id_type=MESH
            )
        for r in range(1, n_heads):
            pl.semaphore_signal(
                barrier, inc=1, device_id={"heads": (h + r) % n_heads}, device_id_type=MESH
            )

        lg_load.wait()
        for step in range(chips):
            w_loads[2 * step].wait()
            w_loads[2 * step + 1].wait()
            product = contract_last(lg_v[...], w_v[step])
            oth_tx[step] = product[:, DH:].astype(BF16)
            mine[step] = product[:, :DH]
        for load in small_loads:
            load.wait()
        pl.semaphore_wait(barrier, n_heads + n_seq - 2)

        oth_copies = [
            to_head(oth_tx.at[i], oth_rx.at[i], oth_send.at[i], oth_recv.at[i], sib)
            for i in range(chips)
        ]
        for copy in oth_copies:
            copy.start()

        def spread_seq(buf, send, recv):
            for r in seq_order:
                to_seq(
                    buf.at[own_rows, :], buf.at[pl.ds(r * part, part), :],
                    send, recv, (s + r) % n_seq,
                ).start()

        spread_seq(k_all, k_send, k_recv)

        c1_copies = []
        for i, r in enumerate(chip_order):
            oth_copies[i].wait_recv()
            total = mine[i] + oth_rx[i].astype(F32)
            if r == 0:
                mine[i] = total
            else:
                c1_tx[i] = total.astype(BF16)
                copy = to_head(
                    c1_tx.at[i], c1_rx.at[i], c1_send.at[i], c1_recv,
                    ((chip + r) % chips) * 2 + core,
                )
                copy.start()
                c1_copies.append(copy)

        def peer(t, q):
            return ((x - t + 4) % 4) * 2 + (core + q) % 2

        def gather_first(buf, send, recv):
            for t in (2, 1, 3):
                to_head(
                    buf.at[j], buf.at[j], send.at[2 * t], recv.at[2 * t],
                    c * GROUP + ((x + t) % 4) * 2 + core,
                ).start()
            to_head(buf.at[j], buf.at[j], send.at[1], recv.at[1], sib).start()

        def gather_wait(buf, recv, t, q):
            await_bytes(buf.at[peer(t, q)], recv.at[2 * t + q])

        def gather_pass(buf, send, recv, t):
            gather_wait(buf, recv, t, 0)
            other = peer(t, 0)
            to_head(
                buf.at[other], buf.at[other], send.at[2 * t + 1], recv.at[2 * t + 1], sib
            ).start()

        gather_first(q_all, q_send, q_recv)
        spread_seq(v_all, v_send, v_recv)

        lane = lax.broadcasted_iota(jnp.int32, (1, ROWS), 1)
        q_pos = jnp.where(
            lane < ROWS // 2,
            bo[2 * s] * (ROWS // 2) + lane,
            bo[2 * s + 1] * (ROWS // 2) + lane - ROWS // 2,
        )
        start1 = dl[0]
        start2 = start1 + dl[1]
        start3 = start2 + dl[2]
        q_begin = jnp.zeros((1, ROWS), jnp.int32)
        for begin in (start1, start2, start3):
            q_begin = jnp.maximum(q_begin, jnp.where(begin <= q_pos, begin, 0))
        for r in range(n_seq):
            slot = (s - r + n_seq) % n_seq
            base = bo[2 * slot + j // 4] * (ROWS // 2) + (j % 4) * part
            k_pos = base + lax.broadcasted_iota(jnp.int32, (part, ROWS), 0)
            allowed = (k_pos <= q_pos) & (k_pos >= q_begin)
            bias[pl.ds(r * part, part), :] = jnp.where(allowed, 0.0, NEG)

        await_bytes(k_all.at[rest, :], k_recv)
        kt_v[...] = k_all[...].astype(F32).T.astype(BF16)

        await_bytes(c1_rx, c1_recv)
        total = mine[chips - 1]
        for i in range(chips - 1):
            total = total + c1_rx[i].astype(F32)
        do_all[j] = total.astype(BF16)
        gather_first(do_all, do_send, do_recv)
        hg_copy = pltpu.make_async_copy(do_all.at[j], hg_out, out_sem.at[0])
        hg_copy.start()

        order = ((0, 0), (0, 1), (1, 0), (3, 0), (2, 0), (1, 1), (3, 1), (2, 1))

        def score_head(head):
            sc = contract_last(k_all[...], q_all[head]) * scale2 + bias[...]
            top = jnp.max(sc, axis=0, keepdims=True)
            e = jnp.exp2(sc - top)
            e_all[head] = e
            st_own[0, pl.ds(head, 1), :] = top
            st_own[1, pl.ds(head, 1), :] = jnp.sum(e, axis=0, keepdims=True)

        for t, q in order:
            if t > 0 and q == 0:
                gather_pass(q_all, q_send, q_recv, t)
            elif q == 1:
                gather_wait(q_all, q_recv, t, q)
            score_head(peer(t, q))

        def group_send(own, rx, send, recv):
            for r in (4, 3, 5, 2, 6, 1, 7):
                to_head(
                    own, rx.at[r - 1], send, recv, c * GROUP + (j + r) % GROUP
                ).start()

        group_send(st_own, st_rx, st_send, st_recv)

        await_bytes(v_all.at[rest, :], v_recv)

        def dot_head(head):
            dp = contract_last(v_all[...], do_all[head])
            dp_all[head] = dp
            d_own[pl.ds(head, 1), :] = jnp.sum(e_all[head] * dp, axis=0, keepdims=True)

        for t, q in order:
            if t > 0 and q == 0:
                gather_pass(do_all, do_send, do_recv, t)
            elif q == 1:
                gather_wait(do_all, do_recv, t, q)
            dot_head(peer(t, q))

        group_send(d_own, d_rx, d_send, d_recv)

        await_bytes(st_rx, st_recv)
        top = st_own[0]
        for r in range(GROUP - 1):
            top = jnp.maximum(top, st_rx[r, 0])
        own_fac = jnp.exp2(st_own[0] - top)
        norm = st_own[1] * own_fac
        for r in range(GROUP - 1):
            norm = norm + st_rx[r, 1] * jnp.exp2(st_rx[r, 0] - top)
        inverse = 1.0 / norm
        own_fac = own_fac * inverse
        fac[...] = own_fac

        dv_acc[...] = jnp.zeros_like(dv_acc)
        for head in range(GROUP):
            p = (e_all[head] * fac[pl.ds(head, 1), :]).astype(BF16)
            dv_acc[...] += matmul(p, do_all[head])
        dv_tx[...] = dv_acc[...].astype(BF16)

        def scatter(tx, rx, send, recv):
            for r in seq_order:
                rows = pl.ds(r * part, part)
                to_seq(
                    tx.at[rows, :], rx.at[rows, :], send, recv, (s - r + n_seq) % n_seq
                ).start()

        scatter(dv_tx, dv_rx, dv_send, dv_recv)

        await_bytes(d_rx, d_recv)
        row_dots = d_own[...] * own_fac
        for r in range(GROUP - 1):
            row_dots = row_dots + d_rx[r] * (jnp.exp2(st_rx[r, 0] - top) * inverse)
        dsum[...] = row_dots

        dk_acc[...] = jnp.zeros_like(dk_acc)
        for head in range(GROUP):
            p = e_all[head] * fac[pl.ds(head, 1), :]
            ds = (p * (dp_all[head] - dsum[pl.ds(head, 1), :])).astype(BF16)
            ds_all[head] = ds
            dk_acc[...] += matmul(ds, q_all[head])
        dk_tx[...] = (dk_acc[...] * scale).astype(BF16)
        scatter(dk_tx, dk_rx, dk_send, dk_recv)

        for t, q in ((2, 0), (2, 1), (1, 0), (1, 1), (3, 0), (3, 1), (0, 1), (0, 0)):
            head = peer(t, q)
            dq_tx[head] = (matmul(kt_v[...], ds_all[head]) * scale).astype(BF16)
            slot = 2 * t + q - 1
            if slot >= 0:
                to_head(
                    dq_tx.at[head], dq_rx.at[slot], dq_send.at[slot], dq_recv, c * GROUP + head
                ).start()

        head_order = (12, 13, 11, 4, 5, 3, 10, 14, 6, 2, 9, 8, 7, 15, 1)

        def finish(tx, rx, fin, out, recv, all_send, all_recv, own_sem):
            await_bytes(rx.at[rest, :], recv)
            summed = tx[own_rows, :].astype(F32)
            for r in range(1, n_seq):
                summed = summed + rx[pl.ds(r * part, part), :].astype(F32)
            fin[...] = summed.astype(BF16)
            place = out.at[pl.ds(row0, part), pl.ds(col0, DH)]
            for r in head_order:
                to_head(fin, place, all_send, all_recv, (h + r) % n_heads).start()
            copy = pltpu.make_async_copy(fin, place, own_sem)
            copy.start()
            return copy

        vg_copy = finish(dv_tx, dv_rx, dv_fin, vg_out, dv_recv, av_send, av_recv, out_sem.at[1])
        kg_copy = finish(dk_tx, dk_rx, dk_fin, kg_out, dk_recv, ak_send, ak_recv, out_sem.at[2])

        await_bytes(dq_rx, dq_recv)
        query_sum = dq_tx[j].astype(F32)
        for r in range(GROUP - 1):
            query_sum = query_sum + dq_rx[r].astype(F32)
        qg_v[...] = query_sum.T.astype(BF16)
        qg_copy = pltpu.make_async_copy(qg_v, qg_out, out_sem.at[3])
        qg_copy.start()

        for slot in range(1, 2 * 4):
            await_bytes(q_all.at[0], q_send.at[slot])
            await_bytes(do_all.at[0], do_send.at[slot])
        for buf, send in ((k_all, k_send), (v_all, v_send), (dv_tx, dv_send), (dk_tx, dk_send)):
            await_bytes(buf.at[rest, :], send)
        for copy in oth_copies:
            copy.wait_send()
        for copy in c1_copies:
            copy.wait_send()
        await_bytes(st_rx, st_send)
        await_bytes(d_rx, d_send)
        for slot in range(GROUP - 1):
            await_bytes(dq_tx.at[0], dq_send.at[slot])
        spread = (n_heads - 1) * part
        for sem in (av_send, ak_send, av_recv, ak_recv):
            await_bytes(q_all.at[pl.ds(0, 5), pl.ds(0, spread // 5), :], sem)
        for copy in (hg_copy, qg_copy, vg_copy, kg_copy):
            copy.wait()

    return kernel


def local(queries, key_rows, value_rows, layer_grad, w_out, block_order, doc_lengths):
    n_seq = lax.axis_size("seq")
    part = ROWS // GROUP
    keys = n_seq * part
    depth = layer_grad.shape[1]
    chips = GROUP
    vmem = pltpu.VMEM
    dma = pltpu.SemaphoreType.DMA
    scratch = [
        vmem((chips, 2 * DH, depth), BF16),
        vmem((ROWS, depth), BF16),
        vmem((GROUP, ROWS, DH), BF16),
        vmem((GROUP, ROWS, DH), BF16),
        vmem((keys, DH), BF16),
        vmem((keys, DH), BF16),
        vmem((DH, keys), BF16),
        vmem((keys, ROWS), F32),
        pltpu.SMEM(block_order.shape, jnp.int32),
        pltpu.SMEM(doc_lengths.shape, jnp.int32),
        vmem((chips, ROWS, DH), F32),
        vmem((chips, ROWS, DH), BF16),
        vmem((chips, ROWS, DH), BF16),
        vmem((chips - 1, ROWS, DH), BF16),
        vmem((chips - 1, ROWS, DH), BF16),
        vmem((GROUP, keys, ROWS), F32),
        vmem((GROUP, keys, ROWS), F32),
        vmem((GROUP, keys, ROWS), BF16),
        vmem((2, GROUP, ROWS), F32),
        vmem((GROUP - 1, 2, GROUP, ROWS), F32),
        vmem((GROUP, ROWS), F32),
        vmem((GROUP - 1, GROUP, ROWS), F32),
        vmem((GROUP, ROWS), F32),
        vmem((GROUP, ROWS), F32),
        vmem((keys, DH), F32),
        vmem((keys, DH), F32),
        vmem((keys, DH), BF16),
        vmem((keys, DH), BF16),
        vmem((keys, DH), BF16),
        vmem((keys, DH), BF16),
        vmem((part, DH), BF16),
        vmem((part, DH), BF16),
        vmem((GROUP, DH, ROWS), BF16),
        vmem((GROUP - 1, DH, ROWS), BF16),
        vmem((ROWS, DH), BF16),
        dma((chips, 2)),
        dma((6,)),
        dma((4,)),
        dma((8,)),
        dma((8,)),
        dma,
        dma,
        dma,
        dma,
        dma((chips,)),
        dma((chips,)),
        dma((chips - 1,)),
        dma,
        dma((8,)),
        dma((8,)),
        dma,
        dma,
        dma,
        dma,
        dma((GROUP - 1,)),
        dma,
        dma,
        dma,
        dma,
        dma,
        dma,
        dma,
        dma,
        dma,
    ]
    anywhere = pl.BlockSpec(memory_space=pl.ANY)
    return pl.pallas_call(
        make_kernel(n_seq),
        out_shape=(
            jax.ShapeDtypeStruct(queries.shape, BF16),
            jax.ShapeDtypeStruct(key_rows.shape, BF16),
            jax.ShapeDtypeStruct(value_rows.shape, BF16),
            jax.ShapeDtypeStruct(queries.shape, BF16),
        ),
        in_specs=[anywhere] * 7,
        out_specs=(anywhere,) * 4,
        scratch_shapes=scratch,
        compiler_params=pltpu.CompilerParams(
            collective_id=0, has_side_effects=True, vmem_limit_bytes=58 * 1024 * 1024
        ),
    )(queries, key_rows, value_rows, layer_grad, w_out, block_order, doc_lengths)


def solution(mesh):
    return jax.shard_map(
        local,
        mesh=mesh,
        in_specs=(
            P("seq", "heads"),
            P("seq", None),
            P("seq", None),
            P("seq", "heads"),
            P(None, "heads"),
            P(),
            P(),
        ),
        out_specs=(P("seq", "heads"), P("seq", None), P("seq", None), P("seq", "heads")),
        check_vma=False,
    )
```

```python
import math

import jax
import jax.numpy as jnp
from jax import lax
from jax.experimental import pallas as pl
from jax.experimental.pallas import tpu as pltpu
from jax.sharding import PartitionSpec as P

GROUP = 8
EARLY = 3
DH = 128
ROWS = 256
MESH = pl.DeviceIdType.MESH
F32 = jnp.float32
BF16 = jnp.bfloat16
NEG = -1e30


def contract_last(left, right):
    return lax.dot_general(
        left, right, (((1,), (1,)), ((), ())), preferred_element_type=F32
    )


def matmul(left, right):
    return jnp.dot(left, right, preferred_element_type=F32)


def make_kernel(n_seq):
    part = ROWS // GROUP
    keys = n_seq * part
    n_heads = 2 * GROUP
    chips = n_heads // 2
    scale = 1.0 / math.sqrt(DH)
    scale2 = scale * math.log2(math.e)

    def kernel(
        q_hbm, k_hbm, v_hbm, lg_hbm, w_hbm, bo_hbm, dl_hbm,
        qg_out, kg_out, vg_out, hg_out,
        w_v, lg_v, q_all, do_all, k_all, v_all, kt_v, bias, bo, dl,
        mine, oth_tx, oth_rx, c1_tx, c1_rx,
        e_all, dp_all, ds_all, st_own, st_rx, d_own, d_rx, fac, dsum,
        dv_acc, dk_acc, dv_tx, dk_tx, dv_rx, dk_rx, dv_fin, dk_fin,
        pair_tx, pair_rx, dq_own, dq_tx, dq_rx, qg_v,
        w_sem, ld_sem, out_sem,
        q_send, q_recv, k_send, k_recv, v_send, v_recv, oth_send, oth_recv, c1_send, c1_recv,
        do_send, do_recv, st_send, st_recv, d_send, d_recv, pair_send, pair_recv, dq_send, dq_recv,
        dv_send, dv_recv, dk_send, dk_recv, av_send, av_recv, ak_send, ak_recv,
    ):
        h = lax.axis_index("heads")
        s = lax.axis_index("seq")
        c = h // GROUP
        j = h % GROUP
        x = j // 2
        core = h % 2
        chip = h // 2
        sib = h + 1 - 2 * core
        seq_order = sorted(range(1, n_seq), key=lambda r: abs(2 * r - n_seq))
        chip_order = (6, 2, 5, 7, 4, 1, 3, 0)
        rest = pl.ds(part, keys - part)

        def to_head(src, dst, send_sem, recv_sem, target):
            return pltpu.make_async_remote_copy(
                src_ref=src, dst_ref=dst, send_sem=send_sem, recv_sem=recv_sem,
                device_id={"heads": target}, device_id_type=MESH,
            )

        def to_seq(src, dst, send_sem, recv_sem, target):
            return pltpu.make_async_remote_copy(
                src_ref=src, dst_ref=dst, send_sem=send_sem, recv_sem=recv_sem,
                device_id={"seq": target}, device_id_type=MESH,
            )

        def await_bytes(ref, sem):
            pltpu.make_async_copy(ref, ref, sem).wait()

        row0 = pl.multiple_of(j * part, part)
        col0 = pl.multiple_of(c * DH, DH)
        own_rows = pl.ds(0, part)
        lg_load = pltpu.make_async_copy(lg_hbm, lg_v, ld_sem.at[0])
        lg_load.start()
        w_loads = []
        for step, r in enumerate(chip_order):
            first = pl.multiple_of(((chip + r) % chips) * 2 * DH, 2 * DH)
            load = pltpu.make_async_copy(
                w_hbm.at[pl.ds(first, 2 * DH), :], w_v.at[step], w_sem.at[step]
            )
            load.start()
            w_loads.append(load)
        barrier = pltpu.get_barrier_semaphore()
        for r in seq_order:
            pl.semaphore_signal(
                barrier, inc=1, device_id={"seq": (s + r) % n_seq}, device_id_type=MESH
            )
        for r in range(1, n_heads):
            pl.semaphore_signal(
                barrier, inc=1, device_id={"heads": (h + r) % n_heads}, device_id_type=MESH
            )

        small_loads = [
            pltpu.make_async_copy(q_hbm, q_all.at[j], ld_sem.at[1]),
            pltpu.make_async_copy(
                k_hbm.at[pl.ds(row0, part), pl.ds(col0, DH)], k_all.at[own_rows, :], ld_sem.at[2]
            ),
            pltpu.make_async_copy(
                v_hbm.at[pl.ds(row0, part), pl.ds(col0, DH)], v_all.at[own_rows, :], ld_sem.at[3]
            ),
            pltpu.make_async_copy(bo_hbm, bo, ld_sem.at[4]),
            pltpu.make_async_copy(dl_hbm, dl, ld_sem.at[5]),
        ]
        for load in small_loads:
            load.start()

        oth_copies = [
            to_head(oth_tx.at[i], oth_rx.at[i], oth_send.at[i], oth_recv.at[i], sib)
            for i in range(chips)
        ]
        c1_copies = []

        def product_step(step):
            w_loads[step].wait()
            product = contract_last(lg_v[...], w_v[step])
            even, odd = product[:, :DH], product[:, DH:]
            oth_tx[step] = jnp.where(core == 0, odd, even).astype(BF16)
            mine[step] = jnp.where(core == 0, even, odd)

        def pair_step(i):
            oth_copies[i].wait_recv()
            total = mine[i] + oth_rx[i].astype(F32)
            r = chip_order[i]
            if r == 0:
                mine[i] = total
            else:
                c1_tx[i] = total.astype(BF16)
                copy = to_head(
                    c1_tx.at[i], c1_rx.at[i], c1_send.at[i], c1_recv,
                    ((chip + r) % chips) * 2 + core,
                )
                copy.start()
                c1_copies.append(copy)

        lg_load.wait()
        for step in range(EARLY):
            product_step(step)
        for load in small_loads:
            load.wait()
        pl.semaphore_wait(barrier, n_heads + n_seq - 2)
        for i in range(EARLY):
            oth_copies[i].start()

        def peer(t, q):
            return ((x - t + 4) % 4) * 2 + (core + q) % 2

        def gather_step(buf, send, recv, t):
            to_head(
                buf.at[j], buf.at[j], send.at[2 * t], recv.at[2 * t],
                c * GROUP + ((x + t) % 4) * 2 + core,
            ).start()

        def gather_far(buf, send, recv):
            gather_step(buf, send, recv, 2)

        def gather_near(buf, send, recv):
            gather_step(buf, send, recv, 1)
            gather_step(buf, send, recv, 3)

        def gather_sibling(buf, send, recv):
            to_head(buf.at[j], buf.at[j], send.at[1], recv.at[1], sib).start()

        def gather_wait(buf, recv, t, q):
            await_bytes(buf.at[peer(t, q)], recv.at[2 * t + q])

        def gather_pass(buf, send, recv, t):
            gather_wait(buf, recv, t, 0)
            other = peer(t, 0)
            to_head(
                buf.at[other], buf.at[other], send.at[2 * t + 1], recv.at[2 * t + 1], sib
            ).start()

        def spread_seq(buf, send, recv):
            for r in seq_order:
                to_seq(
                    buf.at[own_rows, :], buf.at[pl.ds(r * part, part), :],
                    send, recv, (s + r) % n_seq,
                ).start()

        gather_near(q_all, q_send, q_recv)
        spread_seq(k_all, k_send, k_recv)

        for i in range(EARLY, chips):
            product_step(i)
            oth_copies[i].start()
            pair_step(i - EARLY)
        for i in range(chips - EARLY, chips):
            pair_step(i)

        gather_far(q_all, q_send, q_recv)
        gather_sibling(q_all, q_send, q_recv)
        spread_seq(v_all, v_send, v_recv)

        lane = lax.broadcasted_iota(jnp.int32, (1, ROWS), 1)
        q_pos = jnp.where(
            lane < ROWS // 2,
            bo[2 * s] * (ROWS // 2) + lane,
            bo[2 * s + 1] * (ROWS // 2) + lane - ROWS // 2,
        )
        start1 = dl[0]
        start2 = start1 + dl[1]
        start3 = start2 + dl[2]
        q_begin = jnp.zeros((1, ROWS), jnp.int32)
        for begin in (start1, start2, start3):
            q_begin = jnp.maximum(q_begin, jnp.where(begin <= q_pos, begin, 0))
        for r in range(n_seq):
            slot = (s - r + n_seq) % n_seq
            base = bo[2 * slot + j // 4] * (ROWS // 2) + (j % 4) * part
            k_pos = base + lax.broadcasted_iota(jnp.int32, (part, ROWS), 0)
            allowed = (k_pos <= q_pos) & (k_pos >= q_begin)
            bias[pl.ds(r * part, part), :] = jnp.where(allowed, 0.0, NEG)

        await_bytes(k_all.at[rest, :], k_recv)
        kt_v[...] = k_all[...].astype(F32).T.astype(BF16)

        def group_send(own, rx, send, recv):
            for r in (4, 3, 5, 2, 6, 1, 7):
                to_head(
                    own, rx.at[r - 1], send, recv, c * GROUP + (j + r) % GROUP
                ).start()

        order = ((0, 0), (0, 1), (1, 0), (3, 0), (2, 0), (1, 1), (3, 1), (2, 1))

        def score_head(head):
            sc = contract_last(k_all[...], q_all[head]) * scale2 + bias[...]
            top = jnp.max(sc, axis=0, keepdims=True)
            e = jnp.exp2(sc - top)
            e_all[head] = e
            st_own[0, pl.ds(head, 1), :] = top
            st_own[1, pl.ds(head, 1), :] = jnp.sum(e, axis=0, keepdims=True)

        def score_steps(steps):
            for t, q in steps:
                if t > 0 and q == 0:
                    gather_pass(q_all, q_send, q_recv, t)
                elif q == 1:
                    gather_wait(q_all, q_recv, t, q)
                score_head(peer(t, q))

        await_bytes(c1_rx, c1_recv)
        total = mine[chips - 1]
        for i in range(chips - 1):
            total = total + c1_rx[i].astype(F32)
        do_all[j] = total.astype(BF16)
        gather_far(do_all, do_send, do_recv)
        gather_near(do_all, do_send, do_recv)
        gather_sibling(do_all, do_send, do_recv)
        hg_copy = pltpu.make_async_copy(do_all.at[j], hg_out, out_sem.at[0])
        hg_copy.start()

        score_steps(order)

        group_send(st_own, st_rx, st_send, st_recv)

        await_bytes(v_all.at[rest, :], v_recv)

        def dot_head(head):
            dp = contract_last(v_all[...], do_all[head])
            dp_all[head] = dp
            d_own[pl.ds(head, 1), :] = jnp.sum(e_all[head] * dp, axis=0, keepdims=True)

        for t, q in order:
            if t > 0 and q == 0:
                gather_pass(do_all, do_send, do_recv, t)
            elif q == 1:
                gather_wait(do_all, do_recv, t, q)
            dot_head(peer(t, q))

        group_send(d_own, d_rx, d_send, d_recv)

        await_bytes(st_rx, st_recv)
        top = st_own[0]
        for r in range(GROUP - 1):
            top = jnp.maximum(top, st_rx[r, 0])
        own_fac = jnp.exp2(st_own[0] - top)
        norm = st_own[1] * own_fac
        for r in range(GROUP - 1):
            norm = norm + st_rx[r, 1] * jnp.exp2(st_rx[r, 0] - top)
        inverse = 1.0 / norm
        own_fac = own_fac * inverse
        fac[...] = own_fac

        dv_acc[...] = jnp.zeros_like(dv_acc)
        for head in range(GROUP):
            p = (e_all[head] * fac[pl.ds(head, 1), :]).astype(BF16)
            dv_acc[...] += matmul(p, do_all[head])
        dv_tx[...] = dv_acc[...].astype(BF16)

        def scatter(tx, rx, send, recv):
            for r in seq_order:
                rows = pl.ds(r * part, part)
                to_seq(
                    tx.at[rows, :], rx.at[rows, :], send, recv, (s - r + n_seq) % n_seq
                ).start()

        scatter(dv_tx, dv_rx, dv_send, dv_recv)

        await_bytes(d_rx, d_recv)
        row_dots = d_own[...] * own_fac
        for r in range(GROUP - 1):
            row_dots = row_dots + d_rx[r] * (jnp.exp2(st_rx[r, 0] - top) * inverse)
        dsum[...] = row_dots

        dk_acc[...] = jnp.zeros_like(dk_acc)
        for head in range(GROUP):
            p = e_all[head] * fac[pl.ds(head, 1), :]
            ds = (p * (dp_all[head] - dsum[pl.ds(head, 1), :])).astype(BF16)
            ds_all[head] = ds
            dk_acc[...] += matmul(ds, q_all[head])
        dk_tx[...] = (dk_acc[...] * scale).astype(BF16)
        scatter(dk_tx, dk_rx, dk_send, dk_recv)

        def query_part(t, q):
            head = peer(t, q)
            return matmul(kt_v[...], ds_all[head]) * scale

        pair_copies = []
        for t in (2, 1, 3, 0):
            pair_tx[t] = query_part(t, 1).astype(BF16)
            copy = to_head(
                pair_tx.at[t], pair_rx.at[t], pair_send.at[t], pair_recv.at[t], sib
            )
            copy.start()
            pair_copies.append(copy)
        dq_copies = []
        for t, copy in zip((2, 1, 3, 0), pair_copies):
            part_sum = query_part(t, 0)
            copy.wait_recv()
            part_sum = part_sum + pair_rx[t].astype(F32)
            if t == 0:
                dq_own[...] = part_sum
            else:
                dq_tx[t - 1] = part_sum.astype(BF16)
                copy = to_head(
                    dq_tx.at[t - 1], dq_rx.at[t - 1], dq_send.at[t - 1], dq_recv,
                    c * GROUP + peer(t, 0),
                )
                copy.start()
                dq_copies.append(copy)

        head_order = (12, 13, 11, 4, 5, 3, 10, 14, 6, 2, 9, 8, 7, 15, 1)

        def finish(tx, rx, fin, out, recv, all_send, all_recv, own_sem):
            await_bytes(rx.at[rest, :], recv)
            summed = tx[own_rows, :].astype(F32)
            for r in range(1, n_seq):
                summed = summed + rx[pl.ds(r * part, part), :].astype(F32)
            fin[...] = summed.astype(BF16)
            place = out.at[pl.ds(row0, part), pl.ds(col0, DH)]
            for r in head_order:
                to_head(fin, place, all_send, all_recv, (h + r) % n_heads).start()
            copy = pltpu.make_async_copy(fin, place, own_sem)
            copy.start()
            return copy

        vg_copy = finish(dv_tx, dv_rx, dv_fin, vg_out, dv_recv, av_send, av_recv, out_sem.at[1])
        kg_copy = finish(dk_tx, dk_rx, dk_fin, kg_out, dk_recv, ak_send, ak_recv, out_sem.at[2])

        await_bytes(dq_rx, dq_recv)
        query_sum = dq_own[...]
        for r in range(3):
            query_sum = query_sum + dq_rx[r].astype(F32)
        qg_v[...] = query_sum.T.astype(BF16)
        qg_copy = pltpu.make_async_copy(qg_v, qg_out, out_sem.at[3])
        qg_copy.start()

        for slot in range(1, 2 * 4):
            await_bytes(q_all.at[0], q_send.at[slot])
            await_bytes(do_all.at[0], do_send.at[slot])
        for buf, send in ((k_all, k_send), (v_all, v_send)):
            await_bytes(buf.at[rest, :], send)
        for copy in oth_copies + c1_copies + pair_copies:
            copy.wait_send()
        await_bytes(st_rx, st_send)
        await_bytes(d_rx, d_send)
        hg_copy.wait()

        for buf, send in ((dv_tx, dv_send), (dk_tx, dk_send)):
            await_bytes(buf.at[rest, :], send)
        for copy in dq_copies:
            copy.wait_send()
        spread = (n_heads - 1) * part
        for sem in (av_send, ak_send, av_recv, ak_recv):
            await_bytes(q_all.at[pl.ds(0, 5), pl.ds(0, spread // 5), :], sem)
        for copy in (qg_copy, vg_copy, kg_copy):
            copy.wait()

    return kernel


def place_results(*refs):
    sems = refs[-1]
    copies = [
        pltpu.make_async_copy(refs[i], refs[4 + i], sems.at[i]) for i in range(4)
    ]
    for copy in copies:
        copy.start()
    for copy in copies:
        copy.wait()


def local(queries, key_rows, value_rows, layer_grad, w_out, block_order, doc_lengths):
    n_seq = lax.axis_size("seq")
    part = ROWS // GROUP
    keys = n_seq * part
    depth = layer_grad.shape[1]
    chips = GROUP
    vmem = pltpu.VMEM
    dma = pltpu.SemaphoreType.DMA
    scratch = [
        vmem((chips, 2 * DH, depth), BF16),
        vmem((ROWS, depth), BF16),
        vmem((GROUP, ROWS, DH), BF16),
        vmem((GROUP, ROWS, DH), BF16),
        vmem((keys, DH), BF16),
        vmem((keys, DH), BF16),
        vmem((DH, keys), BF16),
        vmem((keys, ROWS), F32),
        pltpu.SMEM(block_order.shape, jnp.int32),
        pltpu.SMEM(doc_lengths.shape, jnp.int32),
        vmem((chips, ROWS, DH), F32),
        vmem((chips, ROWS, DH), BF16),
        vmem((chips, ROWS, DH), BF16),
        vmem((chips - 1, ROWS, DH), BF16),
        vmem((chips - 1, ROWS, DH), BF16),
        vmem((GROUP, keys, ROWS), F32),
        vmem((GROUP, keys, ROWS), F32),
        vmem((GROUP, keys, ROWS), BF16),
        vmem((2, GROUP, ROWS), F32),
        vmem((GROUP - 1, 2, GROUP, ROWS), F32),
        vmem((GROUP, ROWS), F32),
        vmem((GROUP - 1, GROUP, ROWS), F32),
        vmem((GROUP, ROWS), F32),
        vmem((GROUP, ROWS), F32),
        vmem((keys, DH), F32),
        vmem((keys, DH), F32),
        vmem((keys, DH), BF16),
        vmem((keys, DH), BF16),
        vmem((keys, DH), BF16),
        vmem((keys, DH), BF16),
        vmem((part, DH), BF16),
        vmem((part, DH), BF16),
        vmem((4, DH, ROWS), BF16),
        vmem((4, DH, ROWS), BF16),
        vmem((DH, ROWS), F32),
        vmem((3, DH, ROWS), BF16),
        vmem((3, DH, ROWS), BF16),
        vmem((ROWS, DH), BF16),
        dma((chips,)),
        dma((6,)),
        dma((4,)),
        dma((8,)),
        dma((8,)),
        dma,
        dma,
        dma,
        dma,
        dma((chips,)),
        dma((chips,)),
        dma((chips - 1,)),
        dma,
        dma((8,)),
        dma((8,)),
        dma,
        dma,
        dma,
        dma,
        dma((4,)),
        dma((4,)),
        dma((3,)),
        dma,
        dma,
        dma,
        dma,
        dma,
        dma,
        dma,
        dma,
        dma,
    ]
    anywhere = pl.BlockSpec(memory_space=pl.ANY)
    shapes = (
        jax.ShapeDtypeStruct(queries.shape, BF16),
        jax.ShapeDtypeStruct(key_rows.shape, BF16),
        jax.ShapeDtypeStruct(value_rows.shape, BF16),
        jax.ShapeDtypeStruct(queries.shape, BF16),
    )
    results = pl.pallas_call(
        make_kernel(n_seq),
        out_shape=tuple(pltpu.VMEM(shape.shape, BF16) for shape in shapes),
        in_specs=[anywhere] * 7,
        out_specs=(anywhere,) * 4,
        scratch_shapes=scratch,
        compiler_params=pltpu.CompilerParams(
            collective_id=0, has_side_effects=True, vmem_limit_bytes=58 * 1024 * 1024
        ),
    )(queries, key_rows, value_rows, layer_grad, w_out, block_order, doc_lengths)
    return pl.pallas_call(
        place_results,
        out_shape=shapes,
        in_specs=[anywhere] * 4,
        out_specs=(anywhere,) * 4,
        scratch_shapes=[dma((4,))],
        compiler_params=pltpu.CompilerParams(vmem_limit_bytes=58 * 1024 * 1024),
    )(*[pltpu.with_memory_space_constraint(part_out, pltpu.VMEM) for part_out in results])


def solution(mesh):
    return jax.shard_map(
        local,
        mesh=mesh,
        in_specs=(
            P("seq", "heads"),
            P("seq", None),
            P("seq", None),
            P("seq", "heads"),
            P(None, "heads"),
            P(),
            P(),
        ),
        out_specs=(P("seq", "heads"), P("seq", None), P("seq", None), P("seq", "heads")),
        check_vma=False,
    )
```

```python
import math

import jax
import jax.numpy as jnp
from jax import lax
from jax.experimental import pallas as pl
from jax.experimental.pallas import tpu as pltpu
from jax.sharding import PartitionSpec as P

GROUP = 8
EARLY = 3
DH = 128
ROWS = 256
MESH = pl.DeviceIdType.MESH
F32 = jnp.float32
BF16 = jnp.bfloat16
NEG = -1e30


def contract_last(left, right):
    return lax.dot_general(
        left, right, (((1,), (1,)), ((), ())), preferred_element_type=F32
    )


def matmul(left, right):
    return jnp.dot(left, right, preferred_element_type=F32)


def make_kernel(n_seq):
    part = ROWS // GROUP
    keys = n_seq * part
    both = 2 * keys
    n_heads = 2 * GROUP
    chips = n_heads // 2
    scale = 1.0 / math.sqrt(DH)
    scale2 = scale * math.log2(math.e)

    def kernel(
        q_hbm, k_hbm, v_hbm, lg_hbm, w_hbm, bo_hbm, dl_hbm,
        qg_out, kg_out, vg_out, hg_out,
        w_v, lg_v, q_all, do_all, k_all, v_all, kt_v, bias, bo, dl,
        mine, oth_tx, oth_rx, c1_tx, c1_rx,
        e_all, dp_all, ds_all, st_own, st_rx, d_own, d_rx, fac, dsum,
        acc, half_tx, half_rx, dv_tx, dk_tx, dv_rx, dk_rx, dv_fin, dk_fin,
        dq_own, dq_tx, dq_rx, qg_v,
        w_sem, ld_sem, out_sem,
        q_send, q_recv, pair_kv_send, pair_kv_recv, sib_send, sib_recv, k_send, k_recv, v_send, v_recv, oth_send, oth_recv, c1_send, c1_recv,
        do_send, do_recv, st_send, st_recv, d_send, d_recv, half_send, half_recv, dq_send, dq_recv,
        dv_send, dv_recv, dk_send, dk_recv, av_send, av_recv, ak_send, ak_recv,
    ):
        h = lax.axis_index("heads")
        s = lax.axis_index("seq")
        c = h // GROUP
        j = h % GROUP
        x = j // 2
        core = h % 2

        def device(dy, dx, dc):
            return (((c + dy) % 2) * 4 + (x + dx) % 4) * 2 + (core + dc) % 2

        sib = h + 1 - 2 * core
        seq_order = sorted(range(1, n_seq), key=lambda r: abs(2 * r - n_seq))
        across = (2, 1, 3, 0)
        chip_order = [(dy, dx) for dy in (1, 0) for dx in across]
        head_order = [(dy, dx, dc) for dy, dx in chip_order for dc in (1, 0)][:-1]
        rest = pl.ds(part, keys - part)
        spread_rows = pl.ds(0, keys - 2 * part)

        def to_head(src, dst, send_sem, recv_sem, target):
            return pltpu.make_async_remote_copy(
                src_ref=src, dst_ref=dst, send_sem=send_sem, recv_sem=recv_sem,
                device_id={"heads": target}, device_id_type=MESH,
            )

        def to_seq(src, dst, send_sem, recv_sem, target):
            return pltpu.make_async_remote_copy(
                src_ref=src, dst_ref=dst, send_sem=send_sem, recv_sem=recv_sem,
                device_id={"seq": target}, device_id_type=MESH,
            )

        def await_bytes(ref, sem):
            pltpu.make_async_copy(ref, ref, sem).wait()

        row0 = pl.multiple_of(j * part, part)
        col0 = pl.multiple_of(c * DH, DH)
        own_rows = pl.ds(0, part)
        lg_load = pltpu.make_async_copy(lg_hbm, lg_v, ld_sem.at[0])
        lg_load.start()
        w_loads = []
        for step, (dy, dx) in enumerate(chip_order):
            first = pl.multiple_of((device(dy, dx, 0) // 2) * 2 * DH, 2 * DH)
            load = pltpu.make_async_copy(
                w_hbm.at[pl.ds(first, 2 * DH), :], w_v.at[step], w_sem.at[step]
            )
            load.start()
            w_loads.append(load)
        barrier = pltpu.get_barrier_semaphore()
        for r in seq_order:
            pl.semaphore_signal(
                barrier, inc=1, device_id={"seq": (s + r) % n_seq}, device_id_type=MESH
            )
        for r in range(1, n_heads):
            pl.semaphore_signal(
                barrier, inc=1, device_id={"heads": (h + r) % n_heads}, device_id_type=MESH
            )

        small_loads = [
            pltpu.make_async_copy(q_hbm, q_all.at[x], ld_sem.at[1]),
            pltpu.make_async_copy(
                k_hbm.at[pl.ds(row0, part), pl.ds(col0, DH)], k_all.at[own_rows, :], ld_sem.at[2]
            ),
            pltpu.make_async_copy(
                v_hbm.at[pl.ds(row0, part), pl.ds(col0, DH)], v_all.at[own_rows, :], ld_sem.at[3]
            ),
            pltpu.make_async_copy(bo_hbm, bo, ld_sem.at[4]),
            pltpu.make_async_copy(dl_hbm, dl, ld_sem.at[5]),
        ]
        for load in small_loads:
            load.start()

        oth_copies = [
            to_head(oth_tx.at[i], oth_rx.at[i], oth_send.at[i], oth_recv.at[i], sib)
            for i in range(chips)
        ]
        c1_copies = []

        def product_step(step):
            w_loads[step].wait()
            product = contract_last(lg_v[...], w_v[step])
            even, odd = product[:, :DH], product[:, DH:]
            oth_tx[step] = jnp.where(core == 0, odd, even).astype(BF16)
            mine[step] = jnp.where(core == 0, even, odd)

        def pair_step(i):
            oth_copies[i].wait_recv()
            total = mine[i] + oth_rx[i].astype(F32)
            if i == chips - 1:
                mine[i] = total
            else:
                c1_tx[i] = total.astype(BF16)
                copy = to_head(
                    c1_tx.at[i], c1_rx.at[i], c1_send.at[i], c1_recv,
                    device(*chip_order[i], 0),
                )
                copy.start()
                c1_copies.append(copy)

        lg_load.wait()
        for step in range(EARLY):
            product_step(step)
        for load in small_loads:
            load.wait()
        pl.semaphore_wait(barrier, n_heads + n_seq - 2)
        for i in range(EARLY):
            oth_copies[i].start()

        def peer(t):
            return (x - t + 4) % 4

        def gather_far(buf, send, recv):
            to_head(
                buf.at[x], buf.at[x], send.at[2], recv.at[2], device(0, 2, 0)
            ).start()

        def gather_near(buf, send, recv):
            for t in (1, 3):
                to_head(
                    buf.at[x], buf.at[x], send.at[t], recv.at[t], device(0, t, 0)
                ).start()

        def gather_wait(buf, recv, t):
            if t > 0:
                await_bytes(buf.at[peer(t)], recv.at[t])

        y = s % 2
        pair_seq = s + 1 - 2 * y
        pair_slot = (2 * y - 1 + n_seq) % n_seq

        def slot_rows(r):
            return pl.ds(pl.multiple_of(r * part, part), part)

        def pair_copy(buf, send, recv):
            return to_seq(
                buf.at[own_rows, :],
                buf.at[slot_rows((1 - 2 * y + n_seq) % n_seq), :],
                send, recv, pair_seq,
            )

        z_order = sorted(range(2, n_seq, 2), key=lambda r: abs(2 * r - n_seq))

        def spread_own(buf, send, recv):
            for r in z_order:
                to_seq(
                    buf.at[own_rows, :], buf.at[pl.ds(r * part, part), :],
                    send, recv, (s + r) % n_seq,
                ).start()

        def spread_pair(buf, send, recv):
            for r in z_order:
                to_seq(
                    buf.at[slot_rows(pair_slot), :],
                    buf.at[slot_rows((r + 2 * y - 1 + n_seq) % n_seq), :],
                    send, recv, (s + r) % n_seq,
                ).start()

        pair_k = pair_copy(k_all, pair_kv_send.at[0], pair_kv_recv.at[0])
        pair_v = pair_copy(v_all, pair_kv_send.at[1], pair_kv_recv.at[1])
        pair_k.start()
        pair_v.start()
        gather_near(q_all, q_send, q_recv)
        spread_own(k_all, k_send, k_recv)

        for i in range(EARLY, chips):
            product_step(i)
            oth_copies[i].start()
            pair_step(i - EARLY)
        for i in range(chips - EARLY, chips):
            pair_step(i)

        gather_far(q_all, q_send, q_recv)
        pair_k.wait_recv()
        spread_pair(k_all, k_send, k_recv)
        spread_own(v_all, v_send, v_recv)
        pair_v.wait_recv()
        spread_pair(v_all, v_send, v_recv)

        lane = lax.broadcasted_iota(jnp.int32, (1, ROWS), 1)
        q_pos = jnp.where(
            lane < ROWS // 2,
            bo[2 * s] * (ROWS // 2) + lane,
            bo[2 * s + 1] * (ROWS // 2) + lane - ROWS // 2,
        )
        start1 = dl[0]
        start2 = start1 + dl[1]
        start3 = start2 + dl[2]
        q_begin = jnp.zeros((1, ROWS), jnp.int32)
        for begin in (start1, start2, start3):
            q_begin = jnp.maximum(q_begin, jnp.where(begin <= q_pos, begin, 0))
        for side, group_index in enumerate((j, j + 1 - 2 * core)):
            for r in range(n_seq):
                slot = (s - r + n_seq) % n_seq
                base = (
                    bo[2 * slot + group_index // 4] * (ROWS // 2) + (group_index % 4) * part
                )
                k_pos = base + lax.broadcasted_iota(jnp.int32, (part, ROWS), 0)
                allowed = (k_pos <= q_pos) & (k_pos >= q_begin)
                bias[pl.ds(side * keys + r * part, part), :] = jnp.where(allowed, 0.0, NEG)

        mine_rows, other_rows = pl.ds(0, keys), pl.ds(keys, keys)

        def sib_copy(buf, i):
            return to_head(
                buf.at[mine_rows, :], buf.at[other_rows, :],
                sib_send.at[i], sib_recv.at[i], sib,
            )

        sib_k, sib_v = sib_copy(k_all, 0), sib_copy(v_all, 1)
        await_bytes(k_all.at[spread_rows, :], k_recv)
        sib_k.start()

        await_bytes(c1_rx, c1_recv)
        total = mine[chips - 1]
        for i in range(chips - 1):
            total = total + c1_rx[i].astype(F32)
        do_all[x] = total.astype(BF16)
        gather_far(do_all, do_send, do_recv)
        gather_near(do_all, do_send, do_recv)
        hg_copy = pltpu.make_async_copy(do_all.at[x], hg_out, out_sem.at[0])
        hg_copy.start()

        await_bytes(v_all.at[spread_rows, :], v_recv)
        sib_v.start()
        sib_k.wait_recv()

        order = (0, 1, 3, 2)
        for t in order:
            gather_wait(q_all, q_recv, t)
            sc = contract_last(k_all[...], q_all[peer(t)]) * scale2 + bias[...]
            top = jnp.max(sc, axis=0, keepdims=True)
            e = jnp.exp2(sc - top)
            e_all[t] = e
            st_own[pl.ds(peer(t), 1), :] = top
            st_own[pl.ds(4 + peer(t), 1), :] = jnp.sum(e, axis=0, keepdims=True)

        def group_send(own, rx, send, recv):
            for slot, t in enumerate((2, 1, 3)):
                to_head(own, rx.at[slot], send, recv, device(0, t, 0)).start()

        group_send(st_own, st_rx, st_send, st_recv)

        d_own[...] = jnp.zeros_like(d_own)
        sib_v.wait_recv()
        for t in order:
            gather_wait(do_all, do_recv, t)
            dp = contract_last(v_all[...], do_all[peer(t)])
            dp_all[t] = dp
            d_own[pl.ds(peer(t), 1), :] = jnp.sum(e_all[t] * dp, axis=0, keepdims=True)
        group_send(d_own, d_rx, d_send, d_recv)

        await_bytes(st_rx, st_recv)
        tops = [st_own[0:4, :]] + [st_rx[r, 0:4, :] for r in range(3)]
        sums = [st_own[4:8, :]] + [st_rx[r, 4:8, :] for r in range(3)]
        top = jnp.maximum(jnp.maximum(tops[0], tops[1]), jnp.maximum(tops[2], tops[3]))
        scales = [jnp.exp2(item - top) for item in tops]
        norm = sums[0] * scales[0]
        for r in range(1, 4):
            norm = norm + sums[r] * scales[r]
        scales = [item / norm for item in scales]
        fac[...] = scales[0]

        def value_grad(rows):
            total = None
            for t in order:
                p = (e_all[t, rows, :] * fac[pl.ds(peer(t), 1), :]).astype(BF16)
                term = matmul(p, do_all[peer(t)])
                total = term if total is None else total + term
            return total

        half_copies = [
            to_head(half_tx.at[i], half_rx.at[i], half_send.at[i], half_recv.at[i], sib)
            for i in range(2)
        ]
        half_tx[0] = value_grad(other_rows).astype(BF16)
        half_copies[0].start()
        acc[...] = value_grad(mine_rows)
        kt_v[...] = k_all[...].astype(F32).T.astype(BF16)
        half_copies[0].wait_recv()
        dv_tx[...] = (acc[...] + half_rx[0].astype(F32)).astype(BF16)

        def scatter(tx, rx, send, recv):
            for r in seq_order:
                rows = pl.ds(r * part, part)
                to_seq(
                    tx.at[rows, :], rx.at[rows, :], send, recv, (s - r + n_seq) % n_seq
                ).start()

        scatter(dv_tx, dv_rx, dv_send, dv_recv)

        await_bytes(d_rx, d_recv)
        row_dots = d_own[0:4, :] * scales[0]
        for r in range(3):
            row_dots = row_dots + d_rx[r, 0:4, :] * scales[r + 1]
        dsum[...] = row_dots

        def key_grad(rows):
            total = None
            for t in order:
                row = pl.ds(peer(t), 1)
                p = e_all[t, rows, :] * fac[row, :]
                ds = (p * (dp_all[t, rows, :] - dsum[row, :])).astype(BF16)
                ds_all[t, rows, :] = ds
                term = matmul(ds, q_all[peer(t)])
                total = term if total is None else total + term
            return total

        half_tx[1] = key_grad(other_rows).astype(BF16)
        half_copies[1].start()
        acc[...] = key_grad(mine_rows)
        half_copies[1].wait_recv()
        dk_tx[...] = ((acc[...] + half_rx[1].astype(F32)) * scale).astype(BF16)
        scatter(dk_tx, dk_rx, dk_send, dk_recv)

        dq_copies = []
        for t in (2, 1, 3, 0):
            query_part = matmul(kt_v[...], ds_all[t]) * scale
            if t == 0:
                dq_own[...] = query_part
            else:
                dq_tx[t - 1] = query_part.astype(BF16)
                copy = to_head(
                    dq_tx.at[t - 1], dq_rx.at[t - 1], dq_send.at[t - 1], dq_recv,
                    device(0, 4 - t, 0),
                )
                copy.start()
                dq_copies.append(copy)

        def finish(tx, rx, fin, out, recv, all_send, all_recv, own_sem):
            await_bytes(rx.at[rest, :], recv)
            summed = tx[own_rows, :].astype(F32)
            for r in range(1, n_seq):
                summed = summed + rx[pl.ds(r * part, part), :].astype(F32)
            fin[...] = summed.astype(BF16)
            place = out.at[pl.ds(row0, part), pl.ds(col0, DH)]
            for shift in head_order:
                to_head(fin, place, all_send, all_recv, device(*shift)).start()
            copy = pltpu.make_async_copy(fin, place, own_sem)
            copy.start()
            return copy

        vg_copy = finish(dv_tx, dv_rx, dv_fin, vg_out, dv_recv, av_send, av_recv, out_sem.at[1])
        kg_copy = finish(dk_tx, dk_rx, dk_fin, kg_out, dk_recv, ak_send, ak_recv, out_sem.at[2])

        await_bytes(dq_rx, dq_recv)
        query_sum = dq_own[...]
        for r in range(3):
            query_sum = query_sum + dq_rx[r].astype(F32)
        qg_v[...] = query_sum.T.astype(BF16)
        qg_copy = pltpu.make_async_copy(qg_v, qg_out, out_sem.at[3])
        qg_copy.start()

        for t in range(1, 4):
            await_bytes(q_all.at[0], q_send.at[t])
            await_bytes(do_all.at[0], do_send.at[t])
        for buf, send in ((k_all, k_send), (v_all, v_send)):
            await_bytes(buf.at[spread_rows, :], send)
        for copy in [pair_k, pair_v, sib_k, sib_v, *oth_copies, *c1_copies, *half_copies]:
            copy.wait_send()
        await_bytes(st_rx, st_send)
        await_bytes(d_rx, d_send)
        hg_copy.wait()

        for buf, send in ((dv_tx, dv_send), (dk_tx, dk_send)):
            await_bytes(buf.at[rest, :], send)
        for copy in dq_copies:
            copy.wait_send()
        spread = (n_heads - 1) * part
        for sem in (av_send, ak_send, av_recv, ak_recv):
            await_bytes(q_all.at[pl.ds(0, 3), pl.ds(0, spread // 3), :], sem)
        for copy in (qg_copy, vg_copy, kg_copy):
            copy.wait()

    return kernel


def place_results(*refs):
    sems = refs[-1]
    copies = [
        pltpu.make_async_copy(refs[i], refs[4 + i], sems.at[i]) for i in range(4)
    ]
    for copy in copies:
        copy.start()
    for copy in copies:
        copy.wait()


def local(queries, key_rows, value_rows, layer_grad, w_out, block_order, doc_lengths):
    n_seq = lax.axis_size("seq")
    part = ROWS // GROUP
    keys = n_seq * part
    depth = layer_grad.shape[1]
    chips = GROUP
    vmem = pltpu.VMEM
    dma = pltpu.SemaphoreType.DMA
    both = 2 * keys
    scratch = [
        vmem((chips, 2 * DH, depth), BF16),
        vmem((ROWS, depth), BF16),
        vmem((4, ROWS, DH), BF16),
        vmem((4, ROWS, DH), BF16),
        vmem((both, DH), BF16),
        vmem((both, DH), BF16),
        vmem((DH, both), BF16),
        vmem((both, ROWS), F32),
        pltpu.SMEM(block_order.shape, jnp.int32),
        pltpu.SMEM(doc_lengths.shape, jnp.int32),
        vmem((chips, ROWS, DH), F32),
        vmem((chips, ROWS, DH), BF16),
        vmem((chips, ROWS, DH), BF16),
        vmem((chips - 1, ROWS, DH), BF16),
        vmem((chips - 1, ROWS, DH), BF16),
        vmem((4, both, ROWS), F32),
        vmem((4, both, ROWS), F32),
        vmem((4, both, ROWS), BF16),
        vmem((8, ROWS), F32),
        vmem((3, 8, ROWS), F32),
        vmem((8, ROWS), F32),
        vmem((3, 8, ROWS), F32),
        vmem((4, ROWS), F32),
        vmem((4, ROWS), F32),
        vmem((keys, DH), F32),
        vmem((2, keys, DH), BF16),
        vmem((2, keys, DH), BF16),
        vmem((keys, DH), BF16),
        vmem((keys, DH), BF16),
        vmem((keys, DH), BF16),
        vmem((keys, DH), BF16),
        vmem((part, DH), BF16),
        vmem((part, DH), BF16),
        vmem((DH, ROWS), F32),
        vmem((3, DH, ROWS), BF16),
        vmem((3, DH, ROWS), BF16),
        vmem((ROWS, DH), BF16),
        dma((chips,)),
        dma((6,)),
        dma((4,)),
        dma((4,)),
        dma((4,)),
        dma((2,)),
        dma((2,)),
        dma((2,)),
        dma((2,)),
        dma,
        dma,
        dma,
        dma,
        dma((chips,)),
        dma((chips,)),
        dma((chips - 1,)),
        dma,
        dma((4,)),
        dma((4,)),
        dma,
        dma,
        dma,
        dma,
        dma((2,)),
        dma((2,)),
        dma((3,)),
        dma,
        dma,
        dma,
        dma,
        dma,
        dma,
        dma,
        dma,
        dma,
    ]
    anywhere = pl.BlockSpec(memory_space=pl.ANY)
    shapes = (
        jax.ShapeDtypeStruct(queries.shape, BF16),
        jax.ShapeDtypeStruct(key_rows.shape, BF16),
        jax.ShapeDtypeStruct(value_rows.shape, BF16),
        jax.ShapeDtypeStruct(queries.shape, BF16),
    )
    results = pl.pallas_call(
        make_kernel(n_seq),
        out_shape=tuple(pltpu.VMEM(shape.shape, BF16) for shape in shapes),
        in_specs=[anywhere] * 7,
        out_specs=(anywhere,) * 4,
        scratch_shapes=scratch,
        compiler_params=pltpu.CompilerParams(
            collective_id=0, has_side_effects=True, vmem_limit_bytes=58 * 1024 * 1024
        ),
    )(queries, key_rows, value_rows, layer_grad, w_out, block_order, doc_lengths)
    return pl.pallas_call(
        place_results,
        out_shape=shapes,
        in_specs=[anywhere] * 4,
        out_specs=(anywhere,) * 4,
        scratch_shapes=[dma((4,))],
        compiler_params=pltpu.CompilerParams(vmem_limit_bytes=58 * 1024 * 1024),
    )(*[pltpu.with_memory_space_constraint(part_out, pltpu.VMEM) for part_out in results])


def solution(mesh):
    return jax.shard_map(
        local,
        mesh=mesh,
        in_specs=(
            P("seq", "heads"),
            P("seq", None),
            P("seq", None),
            P("seq", "heads"),
            P(None, "heads"),
            P(),
            P(),
        ),
        out_specs=(P("seq", "heads"), P("seq", None), P("seq", None), P("seq", "heads")),
        check_vma=False,
    )
```

```python
import math

import jax
import jax.numpy as jnp
from jax import lax
from jax.experimental import pallas as pl
from jax.experimental.pallas import tpu as pltpu
from jax.sharding import PartitionSpec as P

GROUP = 8
EARLY = 3
DH = 128
ROWS = 256
MESH = pl.DeviceIdType.MESH
F32 = jnp.float32
BF16 = jnp.bfloat16
NEG = -1e30


def contract_last(left, right):
    return lax.dot_general(
        left, right, (((1,), (1,)), ((), ())), preferred_element_type=F32
    )


def matmul(left, right):
    return jnp.dot(left, right, preferred_element_type=F32)


def make_kernel(n_seq):
    part = ROWS // GROUP
    keys = n_seq * part
    both = 2 * keys
    n_heads = 2 * GROUP
    chips = n_heads // 2
    scale = 1.0 / math.sqrt(DH)
    scale2 = scale * math.log2(math.e)

    def kernel(
        q_hbm, k_hbm, v_hbm, lg_hbm, w_hbm, bo_hbm, dl_hbm,
        qg_out, kg_out, vg_out, hg_out,
        w_v, lg_v, q_all, do_all, k_all, v_all, kt_v, bias, bo, dl,
        mine, oth_tx, oth_rx, c1_tx, c1_rx,
        e_all, dp_all, ds_all, st_own, st_rx, d_own, d_rx, fac, dsum,
        acc, half_tx, half_rx, dv_tx, dk_tx, dv_rx, dk_rx, dv_fin, dk_fin,
        dq_own, dq_tx, dq_rx, qg_v,
        w_sem, ld_sem, out_sem,
        q_send, q_recv, pair_kv_send, pair_kv_recv, sib_send, sib_recv, k_send, k_recv, v_send, v_recv, oth_send, oth_recv, c1_send, c1_recv,
        do_send, do_recv, st_send, st_recv, d_send, d_recv, half_send, half_recv, dq_send, dq_recv,
        dv_send, dv_recv, dk_send, dk_recv, av_send, av_recv, ak_send, ak_recv,
    ):
        h = lax.axis_index("heads")
        s = lax.axis_index("seq")
        c = h // GROUP
        j = h % GROUP
        x = j // 2
        core = h % 2

        def device(dy, dx, dc):
            return (((c + dy) % 2) * 4 + (x + dx) % 4) * 2 + (core + dc) % 2

        sib = h + 1 - 2 * core
        seq_order = sorted(range(1, n_seq), key=lambda r: abs(2 * r - n_seq))
        across = (2, 1, 3, 0)
        chip_order = [(dy, dx) for dy in (1, 0) for dx in across]
        head_order = [(dy, dx, dc) for dy, dx in chip_order for dc in (1, 0)][:-1]
        rest = pl.ds(part, keys - part)
        spread_rows = pl.ds(0, keys - 2 * part)

        def to_head(src, dst, send_sem, recv_sem, target):
            return pltpu.make_async_remote_copy(
                src_ref=src, dst_ref=dst, send_sem=send_sem, recv_sem=recv_sem,
                device_id={"heads": target}, device_id_type=MESH,
            )

        def to_seq(src, dst, send_sem, recv_sem, target):
            return pltpu.make_async_remote_copy(
                src_ref=src, dst_ref=dst, send_sem=send_sem, recv_sem=recv_sem,
                device_id={"seq": target}, device_id_type=MESH,
            )

        def await_bytes(ref, sem):
            pltpu.make_async_copy(ref, ref, sem).wait()

        barrier = pltpu.get_barrier_semaphore()
        for r in seq_order:
            pl.semaphore_signal(
                barrier, inc=1, device_id={"seq": (s + r) % n_seq}, device_id_type=MESH
            )
        for r in range(1, n_heads):
            pl.semaphore_signal(
                barrier, inc=1, device_id={"heads": (h + r) % n_heads}, device_id_type=MESH
            )

        row0 = pl.multiple_of(j * part, part)
        col0 = pl.multiple_of(c * DH, DH)
        own_rows = pl.ds(0, part)
        lg_load = pltpu.make_async_copy(lg_hbm, lg_v, ld_sem.at[0])
        lg_load.start()
        w_loads = []
        for step, (dy, dx) in enumerate(chip_order):
            first = pl.multiple_of((device(dy, dx, 0) // 2) * 2 * DH, 2 * DH)
            load = pltpu.make_async_copy(
                w_hbm.at[pl.ds(first, 2 * DH), :], w_v.at[step], w_sem.at[step]
            )
            load.start()
            w_loads.append(load)
        small_loads = [
            pltpu.make_async_copy(q_hbm, q_all.at[x], ld_sem.at[1]),
            pltpu.make_async_copy(
                k_hbm.at[pl.ds(row0, part), pl.ds(col0, DH)], k_all.at[own_rows, :], ld_sem.at[2]
            ),
            pltpu.make_async_copy(
                v_hbm.at[pl.ds(row0, part), pl.ds(col0, DH)], v_all.at[own_rows, :], ld_sem.at[3]
            ),
            pltpu.make_async_copy(bo_hbm, bo, ld_sem.at[4]),
            pltpu.make_async_copy(dl_hbm, dl, ld_sem.at[5]),
        ]
        for load in small_loads:
            load.start()

        oth_copies = [
            to_head(oth_tx.at[i], oth_rx.at[i], oth_send.at[i], oth_recv.at[i], sib)
            for i in range(chips)
        ]
        c1_copies = []

        def product_step(step):
            w_loads[step].wait()
            product = contract_last(lg_v[...], w_v[step])
            even, odd = product[:, :DH], product[:, DH:]
            oth_tx[step] = jnp.where(core == 0, odd, even).astype(BF16)
            mine[step] = jnp.where(core == 0, even, odd)

        def pair_step(i):
            oth_copies[i].wait_recv()
            total = mine[i] + oth_rx[i].astype(F32)
            if i == chips - 1:
                mine[i] = total
            else:
                c1_tx[i] = total.astype(BF16)
                copy = to_head(
                    c1_tx.at[i], c1_rx.at[i], c1_send.at[i], c1_recv,
                    device(*chip_order[i], 0),
                )
                copy.start()
                c1_copies.append(copy)

        lg_load.wait()
        for step in range(EARLY):
            product_step(step)
        for load in small_loads:
            load.wait()
        pl.semaphore_wait(barrier, n_heads + n_seq - 2)
        for i in range(EARLY):
            oth_copies[i].start()

        def peer(t):
            return (x - t + 4) % 4

        def gather_far(buf, send, recv):
            to_head(
                buf.at[x], buf.at[x], send.at[2], recv.at[2], device(0, 2, 0)
            ).start()

        def gather_near(buf, send, recv):
            for t in (1, 3):
                to_head(
                    buf.at[x], buf.at[x], send.at[t], recv.at[t], device(0, t, 0)
                ).start()

        def gather_wait(buf, recv, t):
            if t > 0:
                await_bytes(buf.at[peer(t)], recv.at[t])

        y = s % 2
        pair_seq = s + 1 - 2 * y
        pair_slot = (2 * y - 1 + n_seq) % n_seq

        def slot_rows(r):
            return pl.ds(pl.multiple_of(r * part, part), part)

        def pair_copy(buf, send, recv):
            return to_seq(
                buf.at[own_rows, :],
                buf.at[slot_rows((1 - 2 * y + n_seq) % n_seq), :],
                send, recv, pair_seq,
            )

        z_order = sorted(range(2, n_seq, 2), key=lambda r: abs(2 * r - n_seq))

        def spread_own(buf, send, recv):
            for r in z_order:
                to_seq(
                    buf.at[own_rows, :], buf.at[pl.ds(r * part, part), :],
                    send, recv, (s + r) % n_seq,
                ).start()

        def spread_pair(buf, send, recv):
            for r in z_order:
                to_seq(
                    buf.at[slot_rows(pair_slot), :],
                    buf.at[slot_rows((r + 2 * y - 1 + n_seq) % n_seq), :],
                    send, recv, (s + r) % n_seq,
                ).start()

        pair_k = pair_copy(k_all, pair_kv_send.at[0], pair_kv_recv.at[0])
        pair_v = pair_copy(v_all, pair_kv_send.at[1], pair_kv_recv.at[1])
        pair_k.start()
        pair_v.start()
        gather_near(q_all, q_send, q_recv)
        spread_own(k_all, k_send, k_recv)

        for i in range(EARLY, chips):
            product_step(i)
            oth_copies[i].start()
            pair_step(i - EARLY)
        for i in range(chips - EARLY, chips):
            pair_step(i)

        gather_far(q_all, q_send, q_recv)
        pair_k.wait_recv()
        spread_pair(k_all, k_send, k_recv)
        spread_own(v_all, v_send, v_recv)
        pair_v.wait_recv()
        spread_pair(v_all, v_send, v_recv)

        lane = lax.broadcasted_iota(jnp.int32, (1, ROWS), 1)
        q_pos = jnp.where(
            lane < ROWS // 2,
            bo[2 * s] * (ROWS // 2) + lane,
            bo[2 * s + 1] * (ROWS // 2) + lane - ROWS // 2,
        )
        start1 = dl[0]
        start2 = start1 + dl[1]
        start3 = start2 + dl[2]
        q_begin = jnp.zeros((1, ROWS), jnp.int32)
        for begin in (start1, start2, start3):
            q_begin = jnp.maximum(q_begin, jnp.where(begin <= q_pos, begin, 0))
        for side, group_index in enumerate((j, j + 1 - 2 * core)):
            for r in range(n_seq):
                slot = (s - r + n_seq) % n_seq
                base = (
                    bo[2 * slot + group_index // 4] * (ROWS // 2) + (group_index % 4) * part
                )
                k_pos = base + lax.broadcasted_iota(jnp.int32, (part, ROWS), 0)
                allowed = (k_pos <= q_pos) & (k_pos >= q_begin)
                bias[pl.ds(side * keys + r * part, part), :] = jnp.where(allowed, 0.0, NEG)

        mine_rows, other_rows = pl.ds(0, keys), pl.ds(keys, keys)

        def sib_copy(buf, i):
            return to_head(
                buf.at[mine_rows, :], buf.at[other_rows, :],
                sib_send.at[i], sib_recv.at[i], sib,
            )

        sib_k, sib_v = sib_copy(k_all, 0), sib_copy(v_all, 1)
        await_bytes(k_all.at[spread_rows, :], k_recv)
        sib_k.start()

        await_bytes(c1_rx, c1_recv)
        total = mine[chips - 1]
        for i in range(chips - 1):
            total = total + c1_rx[i].astype(F32)
        do_all[x] = total.astype(BF16)
        gather_far(do_all, do_send, do_recv)
        gather_near(do_all, do_send, do_recv)
        hg_copy = pltpu.make_async_copy(do_all.at[x], hg_out, out_sem.at[0])
        hg_copy.start()

        await_bytes(v_all.at[spread_rows, :], v_recv)
        sib_v.start()
        sib_k.wait_recv()

        order = (0, 1, 3, 2)
        for t in order:
            gather_wait(q_all, q_recv, t)
            sc = contract_last(k_all[...], q_all[peer(t)]) * scale2 + bias[...]
            top = jnp.max(sc, axis=0, keepdims=True)
            e = jnp.exp2(sc - top)
            e_all[t] = e
            st_own[pl.ds(peer(t), 1), :] = top
            st_own[pl.ds(4 + peer(t), 1), :] = jnp.sum(e, axis=0, keepdims=True)

        def group_send(own, rx, send, recv):
            for slot, t in enumerate((2, 1, 3)):
                to_head(own, rx.at[slot], send, recv, device(0, t, 0)).start()

        group_send(st_own, st_rx, st_send, st_recv)

        d_own[...] = jnp.zeros_like(d_own)
        sib_v.wait_recv()
        for t in order:
            gather_wait(do_all, do_recv, t)
            dp = contract_last(v_all[...], do_all[peer(t)])
            dp_all[t] = dp
            d_own[pl.ds(peer(t), 1), :] = jnp.sum(e_all[t] * dp, axis=0, keepdims=True)
        group_send(d_own, d_rx, d_send, d_recv)

        await_bytes(st_rx, st_recv)
        tops = [st_own[0:4, :]] + [st_rx[r, 0:4, :] for r in range(3)]
        sums = [st_own[4:8, :]] + [st_rx[r, 4:8, :] for r in range(3)]
        top = jnp.maximum(jnp.maximum(tops[0], tops[1]), jnp.maximum(tops[2], tops[3]))
        scales = [jnp.exp2(item - top) for item in tops]
        norm = sums[0] * scales[0]
        for r in range(1, 4):
            norm = norm + sums[r] * scales[r]
        scales = [item / norm for item in scales]
        fac[...] = scales[0]

        def value_grad(rows):
            total = None
            for t in order:
                p = e_all[t, rows, :] * fac[pl.ds(peer(t), 1), :]
                e_all[t, rows, :] = p
                term = matmul(p.astype(BF16), do_all[peer(t)])
                total = term if total is None else total + term
            return total

        half_copies = [
            to_head(half_tx.at[i], half_rx.at[i], half_send.at[i], half_recv.at[i], sib)
            for i in range(2)
        ]
        half_tx[0] = value_grad(other_rows).astype(BF16)
        half_copies[0].start()
        acc[...] = value_grad(mine_rows)
        kt_v[...] = k_all[...].astype(F32).T.astype(BF16)
        half_copies[0].wait_recv()
        dv_tx[...] = (acc[...] + half_rx[0].astype(F32)).astype(BF16)

        def scatter(tx, rx, send, recv):
            for r in seq_order:
                rows = pl.ds(r * part, part)
                to_seq(
                    tx.at[rows, :], rx.at[rows, :], send, recv, (s - r + n_seq) % n_seq
                ).start()

        scatter(dv_tx, dv_rx, dv_send, dv_recv)

        await_bytes(d_rx, d_recv)
        row_dots = d_own[0:4, :] * scales[0]
        for r in range(3):
            row_dots = row_dots + d_rx[r, 0:4, :] * scales[r + 1]
        dsum[...] = row_dots

        def key_grad(rows):
            total = None
            for t in order:
                row = pl.ds(peer(t), 1)
                ds = (e_all[t, rows, :] * (dp_all[t, rows, :] - dsum[row, :])).astype(BF16)
                ds_all[t, rows, :] = ds
                term = matmul(ds, q_all[peer(t)])
                total = term if total is None else total + term
            return total

        half_tx[1] = key_grad(other_rows).astype(BF16)
        half_copies[1].start()
        acc[...] = key_grad(mine_rows)
        half_copies[1].wait_recv()
        dk_tx[...] = ((acc[...] + half_rx[1].astype(F32)) * scale).astype(BF16)
        scatter(dk_tx, dk_rx, dk_send, dk_recv)

        dq_copies = []
        for t in (2, 1, 3, 0):
            query_part = matmul(kt_v[...], ds_all[t]) * scale
            if t == 0:
                dq_own[...] = query_part
            else:
                dq_tx[t - 1] = query_part.astype(BF16)
                copy = to_head(
                    dq_tx.at[t - 1], dq_rx.at[t - 1], dq_send.at[t - 1], dq_recv,
                    device(0, 4 - t, 0),
                )
                copy.start()
                dq_copies.append(copy)

        def finish(tx, rx, fin, out, recv, all_send, all_recv, own_sem):
            await_bytes(rx.at[rest, :], recv)
            summed = tx[own_rows, :].astype(F32)
            for r in range(1, n_seq):
                summed = summed + rx[pl.ds(r * part, part), :].astype(F32)
            fin[...] = summed.astype(BF16)
            place = out.at[pl.ds(row0, part), pl.ds(col0, DH)]
            for shift in head_order:
                to_head(fin, place, all_send, all_recv, device(*shift)).start()
            copy = pltpu.make_async_copy(fin, place, own_sem)
            copy.start()
            return copy

        vg_copy = finish(dv_tx, dv_rx, dv_fin, vg_out, dv_recv, av_send, av_recv, out_sem.at[1])
        kg_copy = finish(dk_tx, dk_rx, dk_fin, kg_out, dk_recv, ak_send, ak_recv, out_sem.at[2])

        await_bytes(dq_rx, dq_recv)
        query_sum = dq_own[...]
        for r in range(3):
            query_sum = query_sum + dq_rx[r].astype(F32)
        qg_v[...] = query_sum.T.astype(BF16)
        qg_copy = pltpu.make_async_copy(qg_v, qg_out, out_sem.at[3])
        qg_copy.start()

        for t in range(1, 4):
            await_bytes(q_all.at[0], q_send.at[t])
            await_bytes(do_all.at[0], do_send.at[t])
        for buf, send in ((k_all, k_send), (v_all, v_send)):
            await_bytes(buf.at[spread_rows, :], send)
        for copy in [pair_k, pair_v, sib_k, sib_v, *oth_copies, *c1_copies, *half_copies]:
            copy.wait_send()
        await_bytes(st_rx, st_send)
        await_bytes(d_rx, d_send)
        hg_copy.wait()

        for buf, send in ((dv_tx, dv_send), (dk_tx, dk_send)):
            await_bytes(buf.at[rest, :], send)
        for copy in dq_copies:
            copy.wait_send()
        spread = (n_heads - 1) * part
        for sem in (av_send, ak_send, av_recv, ak_recv):
            await_bytes(q_all.at[pl.ds(0, 3), pl.ds(0, spread // 3), :], sem)
        for copy in (qg_copy, vg_copy, kg_copy):
            copy.wait()

    return kernel


def place_results(*refs):
    sems = refs[-1]
    copies = [
        pltpu.make_async_copy(refs[i], refs[4 + i], sems.at[i]) for i in range(4)
    ]
    for copy in copies:
        copy.start()
    for copy in copies:
        copy.wait()


def local(queries, key_rows, value_rows, layer_grad, w_out, block_order, doc_lengths):
    n_seq = lax.axis_size("seq")
    part = ROWS // GROUP
    keys = n_seq * part
    depth = layer_grad.shape[1]
    chips = GROUP
    vmem = pltpu.VMEM
    dma = pltpu.SemaphoreType.DMA
    both = 2 * keys
    scratch = [
        vmem((chips, 2 * DH, depth), BF16),
        vmem((ROWS, depth), BF16),
        vmem((4, ROWS, DH), BF16),
        vmem((4, ROWS, DH), BF16),
        vmem((both, DH), BF16),
        vmem((both, DH), BF16),
        vmem((DH, both), BF16),
        vmem((both, ROWS), F32),
        pltpu.SMEM(block_order.shape, jnp.int32),
        pltpu.SMEM(doc_lengths.shape, jnp.int32),
        vmem((chips, ROWS, DH), F32),
        vmem((chips, ROWS, DH), BF16),
        vmem((chips, ROWS, DH), BF16),
        vmem((chips - 1, ROWS, DH), BF16),
        vmem((chips - 1, ROWS, DH), BF16),
        vmem((4, both, ROWS), F32),
        vmem((4, both, ROWS), F32),
        vmem((4, both, ROWS), BF16),
        vmem((8, ROWS), F32),
        vmem((3, 8, ROWS), F32),
        vmem((8, ROWS), F32),
        vmem((3, 8, ROWS), F32),
        vmem((4, ROWS), F32),
        vmem((4, ROWS), F32),
        vmem((keys, DH), F32),
        vmem((2, keys, DH), BF16),
        vmem((2, keys, DH), BF16),
        vmem((keys, DH), BF16),
        vmem((keys, DH), BF16),
        vmem((keys, DH), BF16),
        vmem((keys, DH), BF16),
        vmem((part, DH), BF16),
        vmem((part, DH), BF16),
        vmem((DH, ROWS), F32),
        vmem((3, DH, ROWS), BF16),
        vmem((3, DH, ROWS), BF16),
        vmem((ROWS, DH), BF16),
        dma((chips,)),
        dma((6,)),
        dma((4,)),
        dma((4,)),
        dma((4,)),
        dma((2,)),
        dma((2,)),
        dma((2,)),
        dma((2,)),
        dma,
        dma,
        dma,
        dma,
        dma((chips,)),
        dma((chips,)),
        dma((chips - 1,)),
        dma,
        dma((4,)),
        dma((4,)),
        dma,
        dma,
        dma,
        dma,
        dma((2,)),
        dma((2,)),
        dma((3,)),
        dma,
        dma,
        dma,
        dma,
        dma,
        dma,
        dma,
        dma,
        dma,
    ]
    anywhere = pl.BlockSpec(memory_space=pl.ANY)
    shapes = (
        jax.ShapeDtypeStruct(queries.shape, BF16),
        jax.ShapeDtypeStruct(key_rows.shape, BF16),
        jax.ShapeDtypeStruct(value_rows.shape, BF16),
        jax.ShapeDtypeStruct(queries.shape, BF16),
    )
    results = pl.pallas_call(
        make_kernel(n_seq),
        out_shape=tuple(pltpu.VMEM(shape.shape, BF16) for shape in shapes),
        in_specs=[anywhere] * 7,
        out_specs=(anywhere,) * 4,
        scratch_shapes=scratch,
        compiler_params=pltpu.CompilerParams(
            collective_id=0, has_side_effects=True, vmem_limit_bytes=58 * 1024 * 1024
        ),
    )(queries, key_rows, value_rows, layer_grad, w_out, block_order, doc_lengths)
    return pl.pallas_call(
        place_results,
        out_shape=shapes,
        in_specs=[anywhere] * 4,
        out_specs=(anywhere,) * 4,
        scratch_shapes=[dma((4,))],
        compiler_params=pltpu.CompilerParams(vmem_limit_bytes=58 * 1024 * 1024),
    )(*[pltpu.with_memory_space_constraint(part_out, pltpu.VMEM) for part_out in results])


def solution(mesh):
    return jax.shard_map(
        local,
        mesh=mesh,
        in_specs=(
            P("seq", "heads"),
            P("seq", None),
            P("seq", None),
            P("seq", "heads"),
            P(None, "heads"),
            P(),
            P(),
        ),
        out_specs=(P("seq", "heads"), P("seq", None), P("seq", None), P("seq", "heads")),
        check_vma=False,
    )
```

```python
import math

import jax
import jax.numpy as jnp
from jax import lax
from jax.experimental import pallas as pl
from jax.experimental.pallas import tpu as pltpu
from jax.sharding import PartitionSpec as P

GROUP = 8
EARLY = 3
DH = 128
ROWS = 256
MESH = pl.DeviceIdType.MESH
F32 = jnp.float32
BF16 = jnp.bfloat16
NEG = -1e30


def contract_last(left, right):
    return lax.dot_general(
        left, right, (((1,), (1,)), ((), ())), preferred_element_type=F32
    )


def matmul(left, right):
    return jnp.dot(left, right, preferred_element_type=F32)


def make_kernel(n_seq):
    part = ROWS // GROUP
    keys = n_seq * part
    both = 2 * keys
    n_heads = 2 * GROUP
    chips = n_heads // 2
    scale = 1.0 / math.sqrt(DH)
    scale2 = scale * math.log2(math.e)

    def kernel(
        q_hbm, k_hbm, v_hbm, lg_hbm, w_hbm, bo_hbm, dl_hbm,
        qg_out, kg_out, vg_out, hg_out,
        w_v, lg_v, q_all, do_all, k_all, v_all, kt_v, bias, bo, dl,
        mine, oth_tx, oth_rx, c1_tx, c1_rx,
        e_all, dp_all, ds_all, st_own, st_rx, d_own, d_rx, fac, dsum,
        acc, half_tx, half_rx, dv_tx, dk_tx, dv_rx, dk_rx, dv_fin, dk_fin,
        dq_own, dq_tx, dq_rx, qg_v,
        w_sem, ld_sem, out_sem,
        q_send, q_recv, pair_kv_send, pair_kv_recv, sib_send, sib_recv, k_send, k_recv, v_send, v_recv, oth_send, oth_recv, c1_send, c1_recv,
        do_send, do_recv, st_send, st_recv, d_send, d_recv, half_send, half_recv, dq_send, dq_recv,
        dv_send, dv_recv, dk_send, dk_recv, av_send, av_recv, ak_send, ak_recv,
    ):
        h = lax.axis_index("heads")
        s = lax.axis_index("seq")
        c = h // GROUP
        j = h % GROUP
        x = j // 2
        core = h % 2

        def device(dy, dx, dc):
            return (((c + dy) % 2) * 4 + (x + dx) % 4) * 2 + (core + dc) % 2

        sib = h + 1 - 2 * core
        seq_order = sorted(range(1, n_seq), key=lambda r: abs(2 * r - n_seq))
        across = (2, 1, 3, 0)
        chip_order = [(dy, dx) for dy in (1, 0) for dx in across]
        head_order = [(dy, dx, dc) for dy, dx in chip_order for dc in (1, 0)][:-1]
        rest = pl.ds(part, keys - part)
        spread_rows = pl.ds(0, keys - 2 * part)

        def to_head(src, dst, send_sem, recv_sem, target):
            return pltpu.make_async_remote_copy(
                src_ref=src, dst_ref=dst, send_sem=send_sem, recv_sem=recv_sem,
                device_id={"heads": target}, device_id_type=MESH,
            )

        def to_seq(src, dst, send_sem, recv_sem, target):
            return pltpu.make_async_remote_copy(
                src_ref=src, dst_ref=dst, send_sem=send_sem, recv_sem=recv_sem,
                device_id={"seq": target}, device_id_type=MESH,
            )

        def await_bytes(ref, sem):
            pltpu.make_async_copy(ref, ref, sem).wait()

        barrier = pltpu.get_barrier_semaphore()
        for r in seq_order:
            pl.semaphore_signal(
                barrier, inc=1, device_id={"seq": (s + r) % n_seq}, device_id_type=MESH
            )
        for r in range(1, n_heads):
            pl.semaphore_signal(
                barrier, inc=1, device_id={"heads": (h + r) % n_heads}, device_id_type=MESH
            )

        row0 = pl.multiple_of(j * part, part)
        col0 = pl.multiple_of(c * DH, DH)
        own_rows = pl.ds(0, part)
        lg_load = pltpu.make_async_copy(lg_hbm, lg_v, ld_sem.at[0])
        lg_load.start()
        w_loads = []
        for step, (dy, dx) in enumerate(chip_order):
            first = pl.multiple_of((device(dy, dx, 0) // 2) * 2 * DH, 2 * DH)
            load = pltpu.make_async_copy(
                w_hbm.at[pl.ds(first, 2 * DH), :], w_v.at[step], w_sem.at[step]
            )
            load.start()
            w_loads.append(load)
        small_loads = [
            pltpu.make_async_copy(q_hbm, q_all.at[x], ld_sem.at[1]),
            pltpu.make_async_copy(
                k_hbm.at[pl.ds(row0, part), pl.ds(col0, DH)], k_all.at[own_rows, :], ld_sem.at[2]
            ),
            pltpu.make_async_copy(
                v_hbm.at[pl.ds(row0, part), pl.ds(col0, DH)], v_all.at[own_rows, :], ld_sem.at[3]
            ),
            pltpu.make_async_copy(bo_hbm, bo, ld_sem.at[4]),
            pltpu.make_async_copy(dl_hbm, dl, ld_sem.at[5]),
        ]
        for load in small_loads:
            load.start()

        oth_copies = [
            to_head(oth_tx.at[i], oth_rx.at[i], oth_send.at[i], oth_recv.at[i], sib)
            for i in range(chips)
        ]
        c1_copies = []

        def product_step(step):
            w_loads[step].wait()
            product = contract_last(lg_v[...], w_v[step])
            even, odd = product[:, :DH], product[:, DH:]
            oth_tx[step] = jnp.where(core == 0, odd, even).astype(BF16)
            mine[step] = jnp.where(core == 0, even, odd)

        def pair_step(i):
            oth_copies[i].wait_recv()
            total = mine[i] + oth_rx[i].astype(F32)
            if i == chips - 1:
                mine[i] = total
            else:
                c1_tx[i] = total.astype(BF16)
                copy = to_head(
                    c1_tx.at[i], c1_rx.at[i], c1_send.at[i], c1_recv,
                    device(*chip_order[i], 0),
                )
                copy.start()
                c1_copies.append(copy)

        lg_load.wait()
        for step in range(EARLY):
            product_step(step)
        for load in small_loads:
            load.wait()
        pl.semaphore_wait(barrier, n_heads + n_seq - 2)
        for i in range(EARLY):
            oth_copies[i].start()

        def peer(t):
            return (x - t + 4) % 4

        def gather_far(buf, send, recv):
            to_head(
                buf.at[x], buf.at[x], send.at[2], recv.at[2], device(0, 2, 0)
            ).start()

        def gather_near(buf, send, recv):
            for t in (1, 3):
                to_head(
                    buf.at[x], buf.at[x], send.at[t], recv.at[t], device(0, t, 0)
                ).start()

        def gather_wait(buf, recv, t):
            if t > 0:
                await_bytes(buf.at[peer(t)], recv.at[t])

        y = s % 2
        pair_seq = s + 1 - 2 * y
        pair_slot = (2 * y - 1 + n_seq) % n_seq

        def slot_rows(r):
            return pl.ds(pl.multiple_of(r * part, part), part)

        def pair_copy(buf, send, recv):
            return to_seq(
                buf.at[own_rows, :],
                buf.at[slot_rows((1 - 2 * y + n_seq) % n_seq), :],
                send, recv, pair_seq,
            )

        z_order = sorted(range(2, n_seq, 2), key=lambda r: abs(2 * r - n_seq))

        def spread_own(buf, send, recv):
            for r in z_order:
                to_seq(
                    buf.at[own_rows, :], buf.at[pl.ds(r * part, part), :],
                    send, recv, (s + r) % n_seq,
                ).start()

        def spread_pair(buf, send, recv):
            for r in z_order:
                to_seq(
                    buf.at[slot_rows(pair_slot), :],
                    buf.at[slot_rows((r + 2 * y - 1 + n_seq) % n_seq), :],
                    send, recv, (s + r) % n_seq,
                ).start()

        pair_k = pair_copy(k_all, pair_kv_send.at[0], pair_kv_recv.at[0])
        pair_v = pair_copy(v_all, pair_kv_send.at[1], pair_kv_recv.at[1])
        pair_k.start()
        pair_v.start()
        gather_near(q_all, q_send, q_recv)
        spread_own(k_all, k_send, k_recv)

        for i in range(EARLY, chips):
            product_step(i)
            oth_copies[i].start()
            pair_step(i - EARLY)
        for i in range(chips - EARLY, chips):
            pair_step(i)

        gather_far(q_all, q_send, q_recv)
        pair_k.wait_recv()
        spread_pair(k_all, k_send, k_recv)
        spread_own(v_all, v_send, v_recv)
        pair_v.wait_recv()
        spread_pair(v_all, v_send, v_recv)

        lane = lax.broadcasted_iota(jnp.int32, (1, ROWS), 1)
        q_pos = jnp.where(
            lane < ROWS // 2,
            bo[2 * s] * (ROWS // 2) + lane,
            bo[2 * s + 1] * (ROWS // 2) + lane - ROWS // 2,
        )
        start1 = dl[0]
        start2 = start1 + dl[1]
        start3 = start2 + dl[2]
        q_begin = jnp.zeros((1, ROWS), jnp.int32)
        for begin in (start1, start2, start3):
            q_begin = jnp.maximum(q_begin, jnp.where(begin <= q_pos, begin, 0))
        for side, group_index in enumerate((j, j + 1 - 2 * core)):
            for r in range(n_seq):
                slot = (s - r + n_seq) % n_seq
                base = (
                    bo[2 * slot + group_index // 4] * (ROWS // 2) + (group_index % 4) * part
                )
                k_pos = base + lax.broadcasted_iota(jnp.int32, (part, ROWS), 0)
                allowed = (k_pos <= q_pos) & (k_pos >= q_begin)
                bias[pl.ds(side * keys + r * part, part), :] = jnp.where(allowed, 0.0, NEG)

        mine_rows, other_rows = pl.ds(0, keys), pl.ds(keys, keys)

        def sib_copy(buf, i):
            return to_head(
                buf.at[mine_rows, :], buf.at[other_rows, :],
                sib_send.at[i], sib_recv.at[i], sib,
            )

        sib_k, sib_v = sib_copy(k_all, 0), sib_copy(v_all, 1)
        await_bytes(k_all.at[spread_rows, :], k_recv)
        sib_k.start()

        await_bytes(c1_rx, c1_recv)
        total = mine[chips - 1]
        for i in range(chips - 1):
            total = total + c1_rx[i].astype(F32)
        do_all[x] = total.astype(BF16)
        gather_near(do_all, do_send, do_recv)
        gather_far(do_all, do_send, do_recv)
        hg_copy = pltpu.make_async_copy(do_all.at[x], hg_out, out_sem.at[0])
        hg_copy.start()

        await_bytes(v_all.at[spread_rows, :], v_recv)
        sib_v.start()
        sib_k.wait_recv()

        order = (0, 1, 3, 2)
        for t in order:
            gather_wait(q_all, q_recv, t)
            sc = contract_last(k_all[...], q_all[peer(t)]) * scale2 + bias[...]
            top = jnp.max(sc, axis=0, keepdims=True)
            e = jnp.exp2(sc - top)
            e_all[t] = e
            st_own[pl.ds(peer(t), 1), :] = top
            st_own[pl.ds(4 + peer(t), 1), :] = jnp.sum(e, axis=0, keepdims=True)

        def group_send(own, rx, send, recv):
            for slot, t in enumerate((2, 1, 3)):
                to_head(own, rx.at[slot], send, recv, device(0, t, 0)).start()

        group_send(st_own, st_rx, st_send, st_recv)

        d_own[...] = jnp.zeros_like(d_own)
        sib_v.wait_recv()
        for t in order:
            gather_wait(do_all, do_recv, t)
            dp = contract_last(v_all[...], do_all[peer(t)])
            dp_all[t] = dp
            d_own[pl.ds(peer(t), 1), :] = jnp.sum(e_all[t] * dp, axis=0, keepdims=True)
        group_send(d_own, d_rx, d_send, d_recv)

        await_bytes(st_rx, st_recv)
        tops = [st_own[0:4, :]] + [st_rx[r, 0:4, :] for r in range(3)]
        sums = [st_own[4:8, :]] + [st_rx[r, 4:8, :] for r in range(3)]
        top = jnp.maximum(jnp.maximum(tops[0], tops[1]), jnp.maximum(tops[2], tops[3]))
        scales = [jnp.exp2(item - top) for item in tops]
        norm = sums[0] * scales[0]
        for r in range(1, 4):
            norm = norm + sums[r] * scales[r]
        scales = [item / norm for item in scales]
        fac[...] = scales[0]

        def value_grad(rows):
            total = None
            for t in order:
                p = e_all[t, rows, :] * fac[pl.ds(peer(t), 1), :]
                e_all[t, rows, :] = p
                term = matmul(p.astype(BF16), do_all[peer(t)])
                total = term if total is None else total + term
            return total

        half_copies = [
            to_head(half_tx.at[i], half_rx.at[i], half_send.at[i], half_recv.at[i], sib)
            for i in range(2)
        ]
        half_tx[0] = value_grad(other_rows).astype(BF16)
        half_copies[0].start()
        acc[...] = value_grad(mine_rows)
        kt_v[...] = k_all[...].astype(F32).T.astype(BF16)
        half_copies[0].wait_recv()
        dv_tx[...] = (acc[...] + half_rx[0].astype(F32)).astype(BF16)

        def scatter(tx, rx, send, recv):
            for r in seq_order:
                rows = pl.ds(r * part, part)
                to_seq(
                    tx.at[rows, :], rx.at[rows, :], send, recv, (s - r + n_seq) % n_seq
                ).start()

        scatter(dv_tx, dv_rx, dv_send, dv_recv)

        await_bytes(d_rx, d_recv)
        row_dots = d_own[0:4, :] * scales[0]
        for r in range(3):
            row_dots = row_dots + d_rx[r, 0:4, :] * scales[r + 1]
        dsum[...] = row_dots

        def key_grad(rows):
            total = None
            for t in order:
                row = pl.ds(peer(t), 1)
                ds = (e_all[t, rows, :] * (dp_all[t, rows, :] - dsum[row, :])).astype(BF16)
                ds_all[t, rows, :] = ds
                term = matmul(ds, q_all[peer(t)])
                total = term if total is None else total + term
            return total

        half_tx[1] = key_grad(other_rows).astype(BF16)
        half_copies[1].start()
        acc[...] = key_grad(mine_rows)
        half_copies[1].wait_recv()
        dk_tx[...] = ((acc[...] + half_rx[1].astype(F32)) * scale).astype(BF16)
        scatter(dk_tx, dk_rx, dk_send, dk_recv)

        dq_copies = []
        for t in (2, 1, 3, 0):
            query_part = matmul(kt_v[...], ds_all[t]) * scale
            if t == 0:
                dq_own[...] = query_part
            else:
                dq_tx[t - 1] = query_part.astype(BF16)
                copy = to_head(
                    dq_tx.at[t - 1], dq_rx.at[t - 1], dq_send.at[t - 1], dq_recv,
                    device(0, 4 - t, 0),
                )
                copy.start()
                dq_copies.append(copy)

        def finish(tx, rx, fin, out, recv, all_send, all_recv, own_sem):
            await_bytes(rx.at[rest, :], recv)
            summed = tx[own_rows, :].astype(F32)
            for r in range(1, n_seq):
                summed = summed + rx[pl.ds(r * part, part), :].astype(F32)
            fin[...] = summed.astype(BF16)
            place = out.at[pl.ds(row0, part), pl.ds(col0, DH)]
            for shift in head_order:
                to_head(fin, place, all_send, all_recv, device(*shift)).start()
            copy = pltpu.make_async_copy(fin, place, own_sem)
            copy.start()
            return copy

        vg_copy = finish(dv_tx, dv_rx, dv_fin, vg_out, dv_recv, av_send, av_recv, out_sem.at[1])
        kg_copy = finish(dk_tx, dk_rx, dk_fin, kg_out, dk_recv, ak_send, ak_recv, out_sem.at[2])

        await_bytes(dq_rx, dq_recv)
        query_sum = dq_own[...]
        for r in range(3):
            query_sum = query_sum + dq_rx[r].astype(F32)
        qg_v[...] = query_sum.T.astype(BF16)
        qg_copy = pltpu.make_async_copy(qg_v, qg_out, out_sem.at[3])
        qg_copy.start()

        for t in range(1, 4):
            await_bytes(q_all.at[0], q_send.at[t])
            await_bytes(do_all.at[0], do_send.at[t])
        for buf, send in ((k_all, k_send), (v_all, v_send)):
            await_bytes(buf.at[spread_rows, :], send)
        for copy in [pair_k, pair_v, sib_k, sib_v, *oth_copies, *c1_copies, *half_copies]:
            copy.wait_send()
        await_bytes(st_rx, st_send)
        await_bytes(d_rx, d_send)
        hg_copy.wait()

        for buf, send in ((dv_tx, dv_send), (dk_tx, dk_send)):
            await_bytes(buf.at[rest, :], send)
        for copy in dq_copies:
            copy.wait_send()
        spread = (n_heads - 1) * part
        for sem in (av_send, ak_send, av_recv, ak_recv):
            await_bytes(q_all.at[pl.ds(0, 3), pl.ds(0, spread // 3), :], sem)
        for copy in (qg_copy, vg_copy, kg_copy):
            copy.wait()

    return kernel


def place_results(*refs):
    sems = refs[-1]
    copies = [
        pltpu.make_async_copy(refs[i], refs[4 + i], sems.at[i]) for i in range(4)
    ]
    for copy in copies:
        copy.start()
    for copy in copies:
        copy.wait()


def local(queries, key_rows, value_rows, layer_grad, w_out, block_order, doc_lengths):
    n_seq = lax.axis_size("seq")
    part = ROWS // GROUP
    keys = n_seq * part
    depth = layer_grad.shape[1]
    chips = GROUP
    vmem = pltpu.VMEM
    dma = pltpu.SemaphoreType.DMA
    both = 2 * keys
    scratch = [
        vmem((chips, 2 * DH, depth), BF16),
        vmem((ROWS, depth), BF16),
        vmem((4, ROWS, DH), BF16),
        vmem((4, ROWS, DH), BF16),
        vmem((both, DH), BF16),
        vmem((both, DH), BF16),
        vmem((DH, both), BF16),
        vmem((both, ROWS), F32),
        pltpu.SMEM(block_order.shape, jnp.int32),
        pltpu.SMEM(doc_lengths.shape, jnp.int32),
        vmem((chips, ROWS, DH), F32),
        vmem((chips, ROWS, DH), BF16),
        vmem((chips, ROWS, DH), BF16),
        vmem((chips - 1, ROWS, DH), BF16),
        vmem((chips - 1, ROWS, DH), BF16),
        vmem((4, both, ROWS), F32),
        vmem((4, both, ROWS), F32),
        vmem((4, both, ROWS), BF16),
        vmem((8, ROWS), F32),
        vmem((3, 8, ROWS), F32),
        vmem((8, ROWS), F32),
        vmem((3, 8, ROWS), F32),
        vmem((4, ROWS), F32),
        vmem((4, ROWS), F32),
        vmem((keys, DH), F32),
        vmem((2, keys, DH), BF16),
        vmem((2, keys, DH), BF16),
        vmem((keys, DH), BF16),
        vmem((keys, DH), BF16),
        vmem((keys, DH), BF16),
        vmem((keys, DH), BF16),
        vmem((part, DH), BF16),
        vmem((part, DH), BF16),
        vmem((DH, ROWS), F32),
        vmem((3, DH, ROWS), BF16),
        vmem((3, DH, ROWS), BF16),
        vmem((ROWS, DH), BF16),
        dma((chips,)),
        dma((6,)),
        dma((4,)),
        dma((4,)),
        dma((4,)),
        dma((2,)),
        dma((2,)),
        dma((2,)),
        dma((2,)),
        dma,
        dma,
        dma,
        dma,
        dma((chips,)),
        dma((chips,)),
        dma((chips - 1,)),
        dma,
        dma((4,)),
        dma((4,)),
        dma,
        dma,
        dma,
        dma,
        dma((2,)),
        dma((2,)),
        dma((3,)),
        dma,
        dma,
        dma,
        dma,
        dma,
        dma,
        dma,
        dma,
        dma,
    ]
    anywhere = pl.BlockSpec(memory_space=pl.ANY)
    shapes = (
        jax.ShapeDtypeStruct(queries.shape, BF16),
        jax.ShapeDtypeStruct(key_rows.shape, BF16),
        jax.ShapeDtypeStruct(value_rows.shape, BF16),
        jax.ShapeDtypeStruct(queries.shape, BF16),
    )
    results = pl.pallas_call(
        make_kernel(n_seq),
        out_shape=tuple(pltpu.VMEM(shape.shape, BF16) for shape in shapes),
        in_specs=[anywhere] * 7,
        out_specs=(anywhere,) * 4,
        scratch_shapes=scratch,
        compiler_params=pltpu.CompilerParams(
            collective_id=0, has_side_effects=True, vmem_limit_bytes=58 * 1024 * 1024
        ),
    )(queries, key_rows, value_rows, layer_grad, w_out, block_order, doc_lengths)
    return pl.pallas_call(
        place_results,
        out_shape=shapes,
        in_specs=[anywhere] * 4,
        out_specs=(anywhere,) * 4,
        scratch_shapes=[dma((4,))],
        compiler_params=pltpu.CompilerParams(vmem_limit_bytes=58 * 1024 * 1024),
    )(*[pltpu.with_memory_space_constraint(part_out, pltpu.VMEM) for part_out in results])


def solution(mesh):
    return jax.shard_map(
        local,
        mesh=mesh,
        in_specs=(
            P("seq", "heads"),
            P("seq", None),
            P("seq", None),
            P("seq", "heads"),
            P(None, "heads"),
            P(),
            P(),
        ),
        out_specs=(P("seq", "heads"), P("seq", None), P("seq", None), P("seq", "heads")),
        check_vma=False,
    )
```

```python
import math

import jax
import jax.numpy as jnp
from jax import lax
from jax.experimental import pallas as pl
from jax.experimental.pallas import tpu as pltpu
from jax.sharding import PartitionSpec as P

GROUP = 8
EARLY = 3
DH = 128
ROWS = 256
MESH = pl.DeviceIdType.MESH
F32 = jnp.float32
BF16 = jnp.bfloat16
NEG = -1e30


def contract_last(left, right):
    return lax.dot_general(
        left, right, (((1,), (1,)), ((), ())), preferred_element_type=F32
    )


def matmul(left, right):
    return jnp.dot(left, right, preferred_element_type=F32)


def make_kernel(n_seq):
    part = ROWS // GROUP
    keys = n_seq * part
    both = 2 * keys
    n_heads = 2 * GROUP
    chips = n_heads // 2
    scale = 1.0 / math.sqrt(DH)
    scale2 = scale * math.log2(math.e)

    def kernel(
        q_hbm, k_hbm, v_hbm, lg_hbm, w_hbm, bo_hbm, dl_hbm,
        qg_out, kg_out, vg_out, hg_out,
        w_v, lg_v, q_all, do_all, k_all, v_all, kt_v, bias, bo, dl,
        mine, oth_tx, oth_rx, c1_tx, c1_rx,
        e_all, dp_all, ds_all, st_own, st_rx, d_own, d_rx, fac, dsum,
        acc, half_tx, half_rx, dv_tx, dk_tx, dv_rx, dk_rx, dv_fin, dk_fin,
        dq_own, dq_tx, dq_rx, qg_v,
        w_sem, ld_sem, out_sem,
        q_send, q_recv, pair_kv_send, pair_kv_recv, sib_send, sib_recv, k_send, k_recv, v_send, v_recv, oth_send, oth_recv, c1_send, c1_recv,
        do_send, do_recv, st_send, st_recv, d_send, d_recv, half_send, half_recv, dq_send, dq_recv,
        dv_send, dv_recv, dk_send, dk_recv, av_send, av_recv, ak_send, ak_recv,
    ):
        h = lax.axis_index("heads")
        s = lax.axis_index("seq")
        c = h // GROUP
        j = h % GROUP
        x = j // 2
        core = h % 2

        def device(dy, dx, dc):
            return (((c + dy) % 2) * 4 + (x + dx) % 4) * 2 + (core + dc) % 2

        sib = h + 1 - 2 * core
        seq_order = sorted(range(1, n_seq), key=lambda r: abs(2 * r - n_seq))
        across = (2, 1, 3, 0)
        chip_order = [(dy, dx) for dy in (1, 0) for dx in across]
        head_order = [(dy, dx, dc) for dy, dx in chip_order for dc in (1, 0)][:-1]
        rest = pl.ds(part, keys - part)
        spread_rows = pl.ds(0, keys - 2 * part)

        def to_head(src, dst, send_sem, recv_sem, target):
            return pltpu.make_async_remote_copy(
                src_ref=src, dst_ref=dst, send_sem=send_sem, recv_sem=recv_sem,
                device_id={"heads": target}, device_id_type=MESH,
            )

        def to_seq(src, dst, send_sem, recv_sem, target):
            return pltpu.make_async_remote_copy(
                src_ref=src, dst_ref=dst, send_sem=send_sem, recv_sem=recv_sem,
                device_id={"seq": target}, device_id_type=MESH,
            )

        def await_bytes(ref, sem):
            pltpu.make_async_copy(ref, ref, sem).wait()

        barrier = pltpu.get_barrier_semaphore()
        for r in seq_order:
            pl.semaphore_signal(
                barrier, inc=1, device_id={"seq": (s + r) % n_seq}, device_id_type=MESH
            )
        for r in range(1, n_heads):
            pl.semaphore_signal(
                barrier, inc=1, device_id={"heads": (h + r) % n_heads}, device_id_type=MESH
            )

        row0 = pl.multiple_of(j * part, part)
        col0 = pl.multiple_of(c * DH, DH)
        own_rows = pl.ds(0, part)
        lg_load = pltpu.make_async_copy(lg_hbm, lg_v, ld_sem.at[0])
        lg_load.start()
        w_loads = []
        for step, (dy, dx) in enumerate(chip_order):
            first = pl.multiple_of((device(dy, dx, 0) // 2) * 2 * DH, 2 * DH)
            load = pltpu.make_async_copy(
                w_hbm.at[pl.ds(first, 2 * DH), :], w_v.at[step], w_sem.at[step]
            )
            load.start()
            w_loads.append(load)
        small_loads = [
            pltpu.make_async_copy(q_hbm, q_all.at[x], ld_sem.at[1]),
            pltpu.make_async_copy(
                k_hbm.at[pl.ds(row0, part), pl.ds(col0, DH)], k_all.at[own_rows, :], ld_sem.at[2]
            ),
            pltpu.make_async_copy(
                v_hbm.at[pl.ds(row0, part), pl.ds(col0, DH)], v_all.at[own_rows, :], ld_sem.at[3]
            ),
            pltpu.make_async_copy(bo_hbm, bo, ld_sem.at[4]),
            pltpu.make_async_copy(dl_hbm, dl, ld_sem.at[5]),
        ]
        for load in small_loads:
            load.start()

        oth_copies = [
            to_head(oth_tx.at[i], oth_rx.at[i], oth_send.at[i], oth_recv.at[i], sib)
            for i in range(chips)
        ]
        c1_copies = []

        def product_step(step):
            w_loads[step].wait()
            product = contract_last(lg_v[...], w_v[step])
            even, odd = product[:, :DH], product[:, DH:]
            oth_tx[step] = jnp.where(core == 0, odd, even).astype(BF16)
            mine[step] = jnp.where(core == 0, even, odd)

        def pair_step(i):
            oth_copies[i].wait_recv()
            total = mine[i] + oth_rx[i].astype(F32)
            if i == chips - 1:
                mine[i] = total
            else:
                c1_tx[i] = total.astype(BF16)
                copy = to_head(
                    c1_tx.at[i], c1_rx.at[i], c1_send.at[i], c1_recv,
                    device(*chip_order[i], 0),
                )
                copy.start()
                c1_copies.append(copy)

        lg_load.wait()
        for step in range(EARLY):
            product_step(step)
        for load in small_loads:
            load.wait()
        pl.semaphore_wait(barrier, n_heads + n_seq - 2)
        for i in range(EARLY):
            oth_copies[i].start()

        def peer(t):
            return (x - t + 4) % 4

        def gather_far(buf, send, recv):
            to_head(
                buf.at[x], buf.at[x], send.at[2], recv.at[2], device(0, 2, 0)
            ).start()

        def gather_near(buf, send, recv):
            for t in (1, 3):
                to_head(
                    buf.at[x], buf.at[x], send.at[t], recv.at[t], device(0, t, 0)
                ).start()

        def gather_wait(buf, recv, t):
            if t > 0:
                await_bytes(buf.at[peer(t)], recv.at[t])

        y = s % 2
        pair_seq = s + 1 - 2 * y
        pair_slot = (2 * y - 1 + n_seq) % n_seq

        def slot_rows(r):
            return pl.ds(pl.multiple_of(r * part, part), part)

        def pair_copy(buf, send, recv):
            return to_seq(
                buf.at[own_rows, :],
                buf.at[slot_rows((1 - 2 * y + n_seq) % n_seq), :],
                send, recv, pair_seq,
            )

        z_order = sorted(range(2, n_seq, 2), key=lambda r: abs(2 * r - n_seq))

        def spread_own(buf, send, recv):
            for r in z_order:
                to_seq(
                    buf.at[own_rows, :], buf.at[pl.ds(r * part, part), :],
                    send, recv, (s + r) % n_seq,
                ).start()

        def spread_pair(buf, send, recv):
            for r in z_order:
                to_seq(
                    buf.at[slot_rows(pair_slot), :],
                    buf.at[slot_rows((r + 2 * y - 1 + n_seq) % n_seq), :],
                    send, recv, (s + r) % n_seq,
                ).start()

        pair_k = pair_copy(k_all, pair_kv_send.at[0], pair_kv_recv.at[0])
        pair_v = pair_copy(v_all, pair_kv_send.at[1], pair_kv_recv.at[1])
        pair_k.start()
        pair_v.start()
        gather_near(q_all, q_send, q_recv)
        spread_own(k_all, k_send, k_recv)

        for i in range(EARLY, chips):
            product_step(i)
            oth_copies[i].start()
            pair_step(i - EARLY)
        for i in range(chips - EARLY, chips):
            pair_step(i)

        gather_far(q_all, q_send, q_recv)
        pair_k.wait_recv()
        spread_pair(k_all, k_send, k_recv)
        spread_own(v_all, v_send, v_recv)
        pair_v.wait_recv()
        spread_pair(v_all, v_send, v_recv)

        lane = lax.broadcasted_iota(jnp.int32, (1, ROWS), 1)
        q_pos = jnp.where(
            lane < ROWS // 2,
            bo[2 * s] * (ROWS // 2) + lane,
            bo[2 * s + 1] * (ROWS // 2) + lane - ROWS // 2,
        )
        start1 = dl[0]
        start2 = start1 + dl[1]
        start3 = start2 + dl[2]
        q_begin = jnp.zeros((1, ROWS), jnp.int32)
        for begin in (start1, start2, start3):
            q_begin = jnp.maximum(q_begin, jnp.where(begin <= q_pos, begin, 0))
        for side, group_index in enumerate((j, j + 1 - 2 * core)):
            for r in range(n_seq):
                slot = (s - r + n_seq) % n_seq
                base = (
                    bo[2 * slot + group_index // 4] * (ROWS // 2) + (group_index % 4) * part
                )
                k_pos = base + lax.broadcasted_iota(jnp.int32, (part, ROWS), 0)
                allowed = (k_pos <= q_pos) & (k_pos >= q_begin)
                bias[pl.ds(side * keys + r * part, part), :] = jnp.where(allowed, 0.0, NEG)

        mine_rows, other_rows = pl.ds(0, keys), pl.ds(keys, keys)

        def sib_copy(buf, i):
            return to_head(
                buf.at[mine_rows, :], buf.at[other_rows, :],
                sib_send.at[i], sib_recv.at[i], sib,
            )

        sib_k, sib_v = sib_copy(k_all, 0), sib_copy(v_all, 1)
        await_bytes(k_all.at[spread_rows, :], k_recv)
        sib_k.start()

        await_bytes(c1_rx, c1_recv)
        total = mine[chips - 1]
        for i in range(chips - 1):
            total = total + c1_rx[i].astype(F32)
        do_all[x] = total.astype(BF16)
        gather_near(do_all, do_send, do_recv)
        gather_far(do_all, do_send, do_recv)
        hg_copy = pltpu.make_async_copy(do_all.at[x], hg_out, out_sem.at[0])
        hg_copy.start()

        await_bytes(v_all.at[spread_rows, :], v_recv)
        sib_v.start()
        sib_k.wait_recv()

        order = (0, 1, 3, 2)
        for t in order:
            gather_wait(q_all, q_recv, t)
            sc = contract_last(k_all[...], q_all[peer(t)]) * scale2 + bias[...]
            top = jnp.max(sc, axis=0, keepdims=True)
            e = jnp.exp2(sc - top)
            e_all[t] = e
            st_own[pl.ds(peer(t), 1), :] = top
            st_own[pl.ds(4 + peer(t), 1), :] = jnp.sum(e, axis=0, keepdims=True)

        def group_send(own, rx, send, recv):
            for slot, t in enumerate((1, 3, 2)):
                to_head(own, rx.at[slot], send, recv, device(0, t, 0)).start()

        group_send(st_own, st_rx, st_send, st_recv)

        d_own[...] = jnp.zeros_like(d_own)
        sib_v.wait_recv()
        for t in order:
            gather_wait(do_all, do_recv, t)
            dp = contract_last(v_all[...], do_all[peer(t)])
            dp_all[t] = dp
            d_own[pl.ds(peer(t), 1), :] = jnp.sum(e_all[t] * dp, axis=0, keepdims=True)
        group_send(d_own, d_rx, d_send, d_recv)

        await_bytes(st_rx, st_recv)
        tops = [st_own[0:4, :]] + [st_rx[r, 0:4, :] for r in range(3)]
        sums = [st_own[4:8, :]] + [st_rx[r, 4:8, :] for r in range(3)]
        top = jnp.maximum(jnp.maximum(tops[0], tops[1]), jnp.maximum(tops[2], tops[3]))
        scales = [jnp.exp2(item - top) for item in tops]
        norm = sums[0] * scales[0]
        for r in range(1, 4):
            norm = norm + sums[r] * scales[r]
        scales = [item / norm for item in scales]
        fac[...] = scales[0]

        def value_grad(rows):
            total = None
            for t in order:
                p = e_all[t, rows, :] * fac[pl.ds(peer(t), 1), :]
                e_all[t, rows, :] = p
                term = matmul(p.astype(BF16), do_all[peer(t)])
                total = term if total is None else total + term
            return total

        half_copies = [
            to_head(half_tx.at[i], half_rx.at[i], half_send.at[i], half_recv.at[i], sib)
            for i in range(2)
        ]
        half_tx[0] = value_grad(other_rows).astype(BF16)
        half_copies[0].start()
        acc[...] = value_grad(mine_rows)
        kt_v[...] = k_all[...].astype(F32).T.astype(BF16)
        half_copies[0].wait_recv()
        dv_tx[...] = (acc[...] + half_rx[0].astype(F32)).astype(BF16)

        def scatter(tx, rx, send, recv):
            for r in seq_order:
                rows = pl.ds(r * part, part)
                to_seq(
                    tx.at[rows, :], rx.at[rows, :], send, recv, (s - r + n_seq) % n_seq
                ).start()

        scatter(dv_tx, dv_rx, dv_send, dv_recv)

        await_bytes(d_rx, d_recv)
        row_dots = d_own[0:4, :] * scales[0]
        for r in range(3):
            row_dots = row_dots + d_rx[r, 0:4, :] * scales[r + 1]
        dsum[...] = row_dots

        def key_grad(rows):
            total = None
            for t in order:
                row = pl.ds(peer(t), 1)
                ds = (e_all[t, rows, :] * (dp_all[t, rows, :] - dsum[row, :])).astype(BF16)
                ds_all[t, rows, :] = ds
                term = matmul(ds, q_all[peer(t)])
                total = term if total is None else total + term
            return total

        half_tx[1] = key_grad(other_rows).astype(BF16)
        half_copies[1].start()
        acc[...] = key_grad(mine_rows)
        half_copies[1].wait_recv()
        dk_tx[...] = ((acc[...] + half_rx[1].astype(F32)) * scale).astype(BF16)
        scatter(dk_tx, dk_rx, dk_send, dk_recv)

        dq_copies = []
        for t in (2, 1, 3, 0):
            query_part = matmul(kt_v[...], ds_all[t]) * scale
            if t == 0:
                dq_own[...] = query_part
            else:
                dq_tx[t - 1] = query_part.astype(BF16)
                copy = to_head(
                    dq_tx.at[t - 1], dq_rx.at[t - 1], dq_send.at[t - 1], dq_recv,
                    device(0, 4 - t, 0),
                )
                copy.start()
                dq_copies.append(copy)

        def finish(tx, rx, fin, out, recv, all_send, all_recv, own_sem):
            await_bytes(rx.at[rest, :], recv)
            summed = tx[own_rows, :].astype(F32)
            for r in range(1, n_seq):
                summed = summed + rx[pl.ds(r * part, part), :].astype(F32)
            fin[...] = summed.astype(BF16)
            place = out.at[pl.ds(row0, part), pl.ds(col0, DH)]
            for shift in head_order:
                to_head(fin, place, all_send, all_recv, device(*shift)).start()
            copy = pltpu.make_async_copy(fin, place, own_sem)
            copy.start()
            return copy

        vg_copy = finish(dv_tx, dv_rx, dv_fin, vg_out, dv_recv, av_send, av_recv, out_sem.at[1])
        kg_copy = finish(dk_tx, dk_rx, dk_fin, kg_out, dk_recv, ak_send, ak_recv, out_sem.at[2])

        await_bytes(dq_rx, dq_recv)
        query_sum = dq_own[...]
        for r in range(3):
            query_sum = query_sum + dq_rx[r].astype(F32)
        qg_v[...] = query_sum.T.astype(BF16)
        qg_copy = pltpu.make_async_copy(qg_v, qg_out, out_sem.at[3])
        qg_copy.start()

        for t in range(1, 4):
            await_bytes(q_all.at[0], q_send.at[t])
            await_bytes(do_all.at[0], do_send.at[t])
        for buf, send in ((k_all, k_send), (v_all, v_send)):
            await_bytes(buf.at[spread_rows, :], send)
        for copy in [pair_k, pair_v, sib_k, sib_v, *oth_copies, *c1_copies, *half_copies]:
            copy.wait_send()
        await_bytes(st_rx, st_send)
        await_bytes(d_rx, d_send)
        hg_copy.wait()

        for buf, send in ((dv_tx, dv_send), (dk_tx, dk_send)):
            await_bytes(buf.at[rest, :], send)
        for copy in dq_copies:
            copy.wait_send()
        spread = (n_heads - 1) * part
        for sem in (av_send, ak_send, av_recv, ak_recv):
            await_bytes(q_all.at[pl.ds(0, 3), pl.ds(0, spread // 3), :], sem)
        for copy in (qg_copy, vg_copy, kg_copy):
            copy.wait()

    return kernel


def place_results(*refs):
    sems = refs[-1]
    copies = [
        pltpu.make_async_copy(refs[i], refs[4 + i], sems.at[i]) for i in range(4)
    ]
    for copy in copies:
        copy.start()
    for copy in copies:
        copy.wait()


def local(queries, key_rows, value_rows, layer_grad, w_out, block_order, doc_lengths):
    n_seq = lax.axis_size("seq")
    part = ROWS // GROUP
    keys = n_seq * part
    depth = layer_grad.shape[1]
    chips = GROUP
    vmem = pltpu.VMEM
    dma = pltpu.SemaphoreType.DMA
    both = 2 * keys
    scratch = [
        vmem((chips, 2 * DH, depth), BF16),
        vmem((ROWS, depth), BF16),
        vmem((4, ROWS, DH), BF16),
        vmem((4, ROWS, DH), BF16),
        vmem((both, DH), BF16),
        vmem((both, DH), BF16),
        vmem((DH, both), BF16),
        vmem((both, ROWS), F32),
        pltpu.SMEM(block_order.shape, jnp.int32),
        pltpu.SMEM(doc_lengths.shape, jnp.int32),
        vmem((chips, ROWS, DH), F32),
        vmem((chips, ROWS, DH), BF16),
        vmem((chips, ROWS, DH), BF16),
        vmem((chips - 1, ROWS, DH), BF16),
        vmem((chips - 1, ROWS, DH), BF16),
        vmem((4, both, ROWS), F32),
        vmem((4, both, ROWS), F32),
        vmem((4, both, ROWS), BF16),
        vmem((8, ROWS), F32),
        vmem((3, 8, ROWS), F32),
        vmem((8, ROWS), F32),
        vmem((3, 8, ROWS), F32),
        vmem((4, ROWS), F32),
        vmem((4, ROWS), F32),
        vmem((keys, DH), F32),
        vmem((2, keys, DH), BF16),
        vmem((2, keys, DH), BF16),
        vmem((keys, DH), BF16),
        vmem((keys, DH), BF16),
        vmem((keys, DH), BF16),
        vmem((keys, DH), BF16),
        vmem((part, DH), BF16),
        vmem((part, DH), BF16),
        vmem((DH, ROWS), F32),
        vmem((3, DH, ROWS), BF16),
        vmem((3, DH, ROWS), BF16),
        vmem((ROWS, DH), BF16),
        dma((chips,)),
        dma((6,)),
        dma((4,)),
        dma((4,)),
        dma((4,)),
        dma((2,)),
        dma((2,)),
        dma((2,)),
        dma((2,)),
        dma,
        dma,
        dma,
        dma,
        dma((chips,)),
        dma((chips,)),
        dma((chips - 1,)),
        dma,
        dma((4,)),
        dma((4,)),
        dma,
        dma,
        dma,
        dma,
        dma((2,)),
        dma((2,)),
        dma((3,)),
        dma,
        dma,
        dma,
        dma,
        dma,
        dma,
        dma,
        dma,
        dma,
    ]
    anywhere = pl.BlockSpec(memory_space=pl.ANY)
    shapes = (
        jax.ShapeDtypeStruct(queries.shape, BF16),
        jax.ShapeDtypeStruct(key_rows.shape, BF16),
        jax.ShapeDtypeStruct(value_rows.shape, BF16),
        jax.ShapeDtypeStruct(queries.shape, BF16),
    )
    results = pl.pallas_call(
        make_kernel(n_seq),
        out_shape=tuple(pltpu.VMEM(shape.shape, BF16) for shape in shapes),
        in_specs=[anywhere] * 7,
        out_specs=(anywhere,) * 4,
        scratch_shapes=scratch,
        compiler_params=pltpu.CompilerParams(
            collective_id=0, has_side_effects=True, vmem_limit_bytes=58 * 1024 * 1024
        ),
    )(queries, key_rows, value_rows, layer_grad, w_out, block_order, doc_lengths)
    return pl.pallas_call(
        place_results,
        out_shape=shapes,
        in_specs=[anywhere] * 4,
        out_specs=(anywhere,) * 4,
        scratch_shapes=[dma((4,))],
        compiler_params=pltpu.CompilerParams(vmem_limit_bytes=58 * 1024 * 1024),
    )(*[pltpu.with_memory_space_constraint(part_out, pltpu.VMEM) for part_out in results])


def solution(mesh):
    return jax.shard_map(
        local,
        mesh=mesh,
        in_specs=(
            P("seq", "heads"),
            P("seq", None),
            P("seq", None),
            P("seq", "heads"),
            P(None, "heads"),
            P(),
            P(),
        ),
        out_specs=(P("seq", "heads"), P("seq", None), P("seq", None), P("seq", "heads")),
        check_vma=False,
    )
```
